128 devices in a mesh: dp: 32 (over z, x, core), feat: 4 (over y).
Axes of the slice: x: 4, y: 4, z: 4, core: 2. Of those that a mesh axis runs over, the one named last changes fastest.
Arguments:
- samples: bfloat16 [98304, 8192], P('dp', 'feat'), may hold values from -6 to 6
- factors: float32 [256, 8192], P('dp', 'feat'), may hold values from -1 to 1
- weights: float32 [256], replicated, may hold values from 0.2 to 1
- counts: int32 [32], replicated, may hold values from 1024 to 3072, as said below
Outputs:
- gradient: float32 [256, 8192], P('dp', 'feat')
The draws below stay inside these ranges and needn't reach their ends.
Inputs may be any that keep to these rules, and one draw needn't show every extreme that they name: Only the first counts[i] slots of block i are live; some block holds 3072 live samples and some 3072 // 3.
All inputs are finite; a program needn't handle non-finite values.
Results may differ from the reference program's by a relative error of at most 0.0046.
Values may be sent and summed in bfloat16 or wider, within the bound.
No kernel may reach another device: no remote copies, remote signals or barrier semaphores. Data moves between devices by JAX's collectives and lax.ppermute only.
A program may use at most 64 MiB of HBM per device.

```python
import math
import jax
import jax.numpy as jnp
from jax import lax

D = 8192
K = 256
CAP = 3072
SAMPLES = 98304
N_DP = 32


def draw_counts(key, part):
    key = jax.random.fold_in(key, 7)
    first_key, second_key, third_key = jax.random.split(key, 3)
    values = jax.random.randint(first_key, (N_DP,), CAP // 3, CAP + 1)
    fullest = jax.random.randint(second_key, (), 0, N_DP)
    offset = jax.random.randint(third_key, (), 1, N_DP)
    emptiest = (fullest + offset) % N_DP
    values = values.at[fullest].set(CAP)
    values = values.at[emptiest].set(CAP // 3)
    return values.astype(jnp.int32)


def draw_factors(key, part):
    key = jax.random.fold_in(key, 11)
    member_key, center_key, noise_key, share_key = jax.random.split(key, 4)
    cluster_total = max(K // 16, 2)
    member = jax.random.randint(member_key, (K,), 0, cluster_total)
    centers = jax.random.truncated_normal(center_key, -4.0, 4.0, (cluster_total, D), jnp.float32)
    noise = jax.random.truncated_normal(noise_key, -4.0, 4.0, (K, D), jnp.float32)
    share = jax.random.uniform(share_key, (K, 1), jnp.float32, 0.55, 0.85)
    rows = share * centers[member] + jnp.sqrt(1.0 - share * share) * noise
    return (rows * D ** (-0.5)).astype(jnp.float32)


def levels(key, shape, cuts, smallest, top_value):
    level = 1.0
    for dim, blocks in cuts:
        draws = jax.random.uniform(jax.random.fold_in(jax.random.fold_in(key, 6), dim), (blocks,), jnp.float32, smallest / len(cuts), top_value / len(cuts))
        level = level * jnp.repeat(jnp.exp(draws), shape[dim] // blocks).reshape((-1,) + (1,) * (len(shape) - 1 - dim))
    return level


def normal_values(key, extent, width, bound, pieces=(), kind=jnp.bfloat16):
    level = levels(key, extent, pieces, -0.22, 0.18) if pieces else 1.0
    values = jax.random.normal(key, extent, jnp.float32) * width * level
    return jnp.minimum(jnp.maximum(values, -bound), bound).astype(kind)


def setup_inputs(seed: int = 0) -> dict:
    key_of = jax.random.split(jax.random.key(seed), 5)
    return {
        "samples": normal_values(key_of[0], (SAMPLES, D), 1.0, 6.0, ((0, 32), (1, 4))),
        "factors": draw_factors(jax.random.fold_in(key_of[4], 71), 0),
        "weights": jnp.clip(jnp.exp(jax.random.uniform(key_of[2], (K,), jnp.float32, math.log(0.2), math.log(1.0))), 0.2, 1.0),
        "counts": draw_counts(jax.random.fold_in(key_of[4], 71), 0),
    }


def reference(samples, factors, weights, counts):
    narrow = factors.astype(jnp.bfloat16)
    sample_total = jnp.sum(counts).astype(jnp.float32)

    def shard_step(accumulated, shard_number):
        sample_rows = lax.dynamic_slice_in_dim(samples, (shard_number * CAP).astype(jnp.int32), CAP, 0)
        projection = lax.dot_general(sample_rows, narrow, (((1,), (1,)), ((), ())), preferred_element_type=jnp.float32)
        live_rows = (jnp.arange(CAP, dtype=jnp.int32) < counts[shard_number]).astype(jnp.float32)
        cubes_low = (live_rows[:, None] * weights[None, :] * projection ** 3).astype(jnp.bfloat16)
        return accumulated + lax.dot_general(cubes_low, sample_rows, (((0,), (0,)), ((), ())), preferred_element_type=jnp.float32), None

    cross_sum = lax.scan(shard_step, jnp.zeros((K, D), jnp.float32), jnp.arange(N_DP, dtype=jnp.int32))[0]
    gram_matrix = jnp.dot(factors, factors.T, precision=lax.Precision.HIGHEST)
    coupling = weights[:, None] * weights[None, :] * gram_matrix ** 3
    model_term = jnp.dot(coupling, factors, precision=lax.Precision.HIGHEST)
    return 8.0 * model_term - (8.0 / sample_total) * cross_sum
```

```python
import functools

import jax
import jax.numpy as jnp
from jax import lax
from jax.experimental import pallas as pl
from jax.experimental.pallas import tpu as pltpu
from jax.sharding import PartitionSpec as P

BF16 = jnp.bfloat16
F32 = jnp.float32
N_DP = 32
N_FEAT = 4
PLANES = [[2 * chip + core for chip in range(N_DP // 2)] for core in range(2)]


def partner_first(core, y):
    return y ^ 1 if core == 0 else 3 - y


def partner_second(core, y):
    return 3 - y if core == 0 else y ^ 1


def feat_swap(x, partner):
    pairs = []
    for dp in range(N_DP):
        for y in range(N_FEAT):
            pairs.append((dp * N_FEAT + y, dp * N_FEAT + partner(dp % 2, y)))
    return lax.ppermute(x, ("dp", "feat"), pairs)


def core_swap(x):
    return lax.ppermute(x, "dp", [(i, i ^ 1) for i in range(N_DP)])


def plane_exchange(x):
    return lax.all_to_all(x, "dp", 0, 0, axis_index_groups=PLANES, tiled=True)


def projection_kernel(order, other, own, samples, sent0, kept0, sent1, kept1, rows):
    quarter = other.shape[0] // 4

    @pl.when(pl.program_id(0) == 0)
    def _():
        for c, ref in enumerate((other, own)):
            for i in range(4):
                start = pl.multiple_of(order[i] * quarter, quarter)
                rows[pl.ds((4 * c + i) * quarter, quarter), :] = ref[pl.ds(start, quarter), :]

    value = lax.dot_general(
        rows[...], samples[...], (((1,), (1,)), ((), ())), preferred_element_type=F32
    )
    sent0[...] = value[: 2 * quarter].astype(BF16)
    kept0[...] = value[2 * quarter : 4 * quarter]
    sent1[...] = value[4 * quarter : 6 * quarter].astype(BF16)
    kept1[...] = value[6 * quarter :]


def project(order, other, own, samples, tile=512):
    slots, depth = samples.shape
    half = other.shape[0] // 2
    whole = pl.BlockSpec((2 * half, depth), lambda i, s: (0, 0))
    out = pl.BlockSpec((half, tile), lambda i, s: (0, i))
    return pl.pallas_call(
        projection_kernel,
        grid_spec=pltpu.PrefetchScalarGridSpec(
            num_scalar_prefetch=1,
            grid=(slots // tile,),
            in_specs=[whole, whole, pl.BlockSpec((tile, depth), lambda i, s: (i, 0))],
            out_specs=[out] * 4,
            scratch_shapes=[pltpu.VMEM((4 * half, depth), BF16)],
        ),
        out_shape=[
            jax.ShapeDtypeStruct((half, slots), BF16),
            jax.ShapeDtypeStruct((half, slots), F32),
            jax.ShapeDtypeStruct((half, slots), BF16),
            jax.ShapeDtypeStruct((half, slots), F32),
        ],
        compiler_params=pltpu.CompilerParams(vmem_limit_bytes=32 << 20),
        cost_estimate=pl.CostEstimate(
            flops=2 * slots * depth * 4 * half, bytes_accessed=slots * depth * 2, transcendentals=0
        ),
        name="projection",
    )(order, other, own, samples)


def cross_kernel(add, order, cubes0, cubes1, cubes2, samples, *refs):
    if add:
        extra, out, rows = refs
    else:
        out, rows = refs
    quarter = cubes0.shape[0]

    @pl.when(pl.program_id(0) == 0)
    def _():
        pieces = (cubes2[:quarter], cubes2[quarter:], cubes0[...], cubes1[...])
        for i, piece in enumerate(pieces):
            rows[pl.ds(pl.multiple_of(order[i] * quarter, quarter), quarter), :] = piece

    value = lax.dot_general(
        rows[...], samples[...], (((1,), (0,)), ((), ())), preferred_element_type=F32
    )
    if add:
        value = value + extra[...].astype(F32)
    out[...] = value.astype(BF16)


def cross(order, cubes0, cubes1, cubes2, samples, extra=None, tile=512):
    slots, depth = samples.shape
    quarter = cubes0.shape[0]
    add = extra is not None
    one = pl.BlockSpec((quarter, slots), lambda i, s: (0, 0))
    two = pl.BlockSpec((2 * quarter, slots), lambda i, s: (0, 0))
    out = pl.BlockSpec((4 * quarter, tile), lambda i, s: (0, i))
    return pl.pallas_call(
        functools.partial(cross_kernel, add),
        grid_spec=pltpu.PrefetchScalarGridSpec(
            num_scalar_prefetch=1,
            grid=(depth // tile,),
            in_specs=[one, one, two, pl.BlockSpec((slots, tile), lambda i, s: (0, i))]
            + [out] * add,
            out_specs=out,
            scratch_shapes=[pltpu.VMEM((4 * quarter, slots), BF16)],
        ),
        out_shape=jax.ShapeDtypeStruct((4 * quarter, depth), BF16),
        compiler_params=pltpu.CompilerParams(vmem_limit_bytes=32 << 20),
        cost_estimate=pl.CostEstimate(
            flops=2 * slots * depth * 4 * quarter, bytes_accessed=slots * depth * 2, transcendentals=0
        ),
        name="cross",
    )(order, cubes0, cubes1, cubes2, samples, *([extra] if add else []))


def split_dot(left, right, dims):
    high = left.astype(BF16)
    low = (left - high.astype(F32)).astype(BF16)
    both = lax.dot_general(
        jnp.concatenate([high, low], 0), right, (dims, ((), ())), preferred_element_type=F32
    )
    return both[: left.shape[0]] + both[left.shape[0] :]


def on_device(samples, factors, weights, counts):
    owned, depth = factors.shape
    slots = samples.shape[0]
    half_rows = weights.shape[0] // 2
    quarter = half_rows // 4
    dp = lax.axis_index("dp")
    y = lax.axis_index("feat")
    core = lax.rem(dp, 2)
    chip = dp // 2
    first = jnp.where(core == 0, y ^ 1, 3 - y)
    second = jnp.where(core == 0, 3 - y, y ^ 1)
    order = jnp.stack([first, lax.rem(y + 2, 4), y, second]).astype(jnp.int32)
    total = jnp.sum(counts).astype(F32)

    narrow = factors.astype(BF16)
    own = plane_exchange(jnp.tile(narrow, (N_DP // 2, 1)))
    other = core_swap(own)

    sent0, kept0, sent1, kept1 = project(order, other, own, samples)

    by_core = weights.reshape(N_DP // 2, 2, owned).transpose(1, 0, 2).reshape(2, half_rows)
    live = (lax.iota(jnp.int32, slots) < counts[dp]).astype(F32)[None, :]

    def cubes_of(sent, kept, chunk):
        got = feat_swap(sent, partner_first).astype(F32)
        passed = feat_swap((kept[quarter:] + got[quarter:]).astype(BF16), partner_second)
        value = kept[:quarter] + got[:quarter] + passed.astype(F32)
        weight = lax.dynamic_slice(by_core, (chunk, y * quarter), (1, quarter))[0]
        cubes0 = (live * weight[:, None] * value**3).astype(BF16)
        cubes1 = feat_swap(cubes0, partner_second)
        cubes2 = feat_swap(jnp.concatenate([cubes0, cubes1], 0), partner_first)
        return cubes0, cubes1, cubes2

    cubes_other = cubes_of(sent0, kept0, 1 - core)
    cubes_own = cubes_of(sent1, kept1, core)
    cross_other = core_swap(cross(order, *cubes_other, samples))
    cross_own = cross(order, *cubes_own, samples, extra=cross_other)
    blocks = plane_exchange(cross_own).reshape(N_DP // 2, owned, depth)
    cross_term = jnp.sum(blocks.astype(F32), axis=0)

    gram = jnp.concatenate(
        [split_dot(factors, own, ((1,), (1,))), split_dot(factors, other, ((1,), (1,)))], 1
    )
    gram = gram + feat_swap(gram, partner_first)
    gram = gram + feat_swap(gram, partner_second)
    weight_own = lax.dynamic_slice(by_core, (core, 0), (1, half_rows))
    weight_other = lax.dynamic_slice(by_core, (1 - core, 0), (1, half_rows))
    weight_mine = lax.dynamic_slice(weight_own, (0, chip * owned), (1, owned))[0]
    coupling = weight_mine[:, None] * jnp.concatenate([weight_own, weight_other], 1) * gram**3
    mine = lax.broadcasted_iota(jnp.int32, coupling.shape, 0) + chip * owned
    here = lax.broadcasted_iota(jnp.int32, coupling.shape, 1) == mine
    diagonal = jnp.sum(jnp.where(here, coupling, 0.0), 1, keepdims=True)
    model_term = (
        split_dot(coupling[:, :half_rows], own, ((1,), (0,)))
        + split_dot(coupling[:, half_rows:], other, ((1,), (0,)))
        + diagonal * (factors - narrow.astype(F32))
    )
    return 8.0 * model_term - 8.0 / total * cross_term


def solution(mesh):
    in_specs = (P("dp", "feat"), P("dp", "feat"), P(), P())
    out_specs = P("dp", "feat")
    return jax.shard_map(
        on_device, mesh=mesh, in_specs=in_specs, out_specs=out_specs, check_vma=False
    )
```

```python
import functools

import jax
import jax.numpy as jnp
from jax import lax
from jax.experimental import pallas as pl
from jax.experimental.pallas import tpu as pltpu
from jax.sharding import PartitionSpec as P

BF16 = jnp.bfloat16
F32 = jnp.float32
N_DP = 32
N_FEAT = 4
CHIPS = N_DP // 2
PARTS = 2
TILES = (768, 768)
LOADS = 2
PLANES = [[2 * chip + core for chip in range(CHIPS)] for core in range(2)]
VMEM = pl.BlockSpec(memory_space=pltpu.VMEM)
SMEM = pl.BlockSpec(memory_space=pltpu.SMEM)
ANY = pl.BlockSpec(memory_space=pl.ANY)
PARAMS = pltpu.CompilerParams(vmem_limit_bytes=8 << 20)


def in_hbm(array):
    return pltpu.with_memory_space_constraint(array, pltpu.HBM)


def in_vmem(array):
    return pltpu.with_memory_space_constraint(array, pltpu.VMEM)


def partner_first(core, y):
    return y ^ 1 if core == 0 else 3 - y


def partner_second(core, y):
    return 3 - y if core == 0 else y ^ 1


PARTNERS = (partner_first, partner_second)
ALTERNATE = False


def feat_swap(x, partner):
    pairs = []
    for dp in range(N_DP):
        for y in range(N_FEAT):
            pairs.append((dp * N_FEAT + y, dp * N_FEAT + partner(dp % 2, y)))
    return lax.ppermute(x, ("dp", "feat"), pairs)


def core_swap(x):
    return lax.ppermute(x, "dp", [(i, i ^ 1) for i in range(N_DP)])


def plane_exchange(x):
    return lax.all_to_all(x, "dp", 0, 0, axis_index_groups=PLANES, tiled=True)


def spread_kernel(factors, out):
    width = out.shape[1]
    block = jnp.concatenate([factors[:, :width], factors[:, width:]], 0).astype(BF16)
    for chip in range(CHIPS):
        out[pl.ds(16 * chip, 16), :] = block


def spread(factors):
    return pl.pallas_call(
        spread_kernel,
        in_specs=[VMEM],
        out_specs=VMEM,
        out_shape=jax.ShapeDtypeStruct((16 * CHIPS, factors.shape[1] // 2), BF16),
        compiler_params=PARAMS,
        name="spread",
    )(in_hbm(factors))


def unpack(packed, out, top):
    for pair in range(CHIPS // 2):
        block = packed[pl.ds(32 * pair, 32), :].astype(F32)
        upper = jnp.concatenate([block[:8], block[8:16]], 1)
        lower = jnp.concatenate([block[16:24], block[24:]], 1)
        out[pl.ds(top + 16 * pair, 16), :] = jnp.concatenate([upper, lower], 0).astype(BF16)


def parts_of(value):
    high = value.astype(BF16)
    return high, (value - high.astype(F32)).astype(BF16)


def gram_message(gram):
    return jnp.concatenate([part.astype(F32) for part in parts_of(gram)], 0).astype(BF16)


def gram_of(message):
    value = message.astype(F32)
    return value[:8] + value[8:16]


def load_kernel(samples, near, sem):
    rows = near.shape[0] // LOADS
    copies = []
    for i in range(LOADS):
        part = pl.ds(i * rows, rows)
        copies.append(pltpu.make_async_copy(samples.at[part, :], near.at[part, :], sem.at[i]))
        copies[-1].start()
    for copy in copies:
        copy.wait()


def load(samples):
    shape = (samples.shape[0] // PARTS, samples.shape[1])
    return pl.pallas_call(
        load_kernel,
        in_specs=[ANY],
        out_specs=VMEM,
        out_shape=pltpu.VMEM(shape, samples.dtype),
        scratch_shapes=[pltpu.SemaphoreType.DMA((LOADS,))],
        compiler_params=PARAMS,
        cost_estimate=pl.CostEstimate(
            flops=0, bytes_accessed=4 * shape[0] * shape[1], transcendentals=0
        ),
        name="load",
    )(in_hbm(samples))


def arrange(scalars, rows, scratch, pattern):
    block = rows.shape[0] // 4
    for i in range(4):
        at = pl.multiple_of(scalars[4 * pattern + i] * block, block)
        scratch[i * block : (i + 1) * block, :] = rows[pl.ds(at, block), :]


def project_part(scalars, scratch, near, sent, kept, top):
    half = kept.shape[0]
    start = 0
    for tile in TILES:
        rows = slice(start, start + tile)
        value = lax.dot_general(
            scratch[...], near[rows, :], (((1,), (1,)), ((), ())), preferred_element_type=F32
        )
        slot = top + start + lax.broadcasted_iota(jnp.int32, (1, tile), 1)
        value = jnp.where(slot < scalars[8], value, 0.0)
        sent[:, rows] = value[:half].astype(BF16)
        kept[:, rows] = value[half:]
        start += tile


def first_kernel(scalars, packed_other, packed_own, factors, near, samples, *refs):
    sent, kept, rows, gram, later, scratch, mine, sem, sems = refs
    first = pltpu.make_async_copy(factors, mine, sem)
    first.start()
    slots = kept.shape[1]
    copies = []
    for i in range(LOADS):
        part = pl.ds(i * slots // LOADS, slots // LOADS)
        rest = pl.ds(slots + i * slots // LOADS, slots // LOADS)
        copies.append(
            pltpu.make_async_copy(samples.at[rest, :], later.at[part, :], sems.at[i])
        )
        copies[-1].start()
    unpack(packed_other, rows, 0)
    unpack(packed_own, rows, rows.shape[0] // 2)
    arrange(scalars, rows, scratch, 0)
    first.wait()
    value = gram_of(
        lax.dot_general(
            gram_message(mine[...]),
            rows[...],
            (((1,), (1,)), ((), ())),
            preferred_element_type=F32,
        )
    )
    gram[...] = value
    sent[16:, slots:] = jnp.zeros((sent.shape[0] - 16, value.shape[1]), BF16)
    sent[:16, slots:] = gram_message(value)
    project_part(scalars, scratch, near, sent, kept, 0)
    for copy in copies:
        copy.wait()


def second_kernel(scalars, rows, near, sent, kept, scratch, *, pattern):
    arrange(scalars, rows, scratch, pattern)
    project_part(scalars, scratch, near, sent, kept, kept.shape[1])


def estimate(slots, depth, rows):
    return pl.CostEstimate(
        flops=2 * slots * depth * rows, bytes_accessed=2 * slots * depth, transcendentals=0
    )


def project_first(scalars, packed_other, packed_own, factors, near, samples):
    slots, depth = near.shape
    rows = packed_own.shape[0]
    return pl.pallas_call(
        first_kernel,
        in_specs=[SMEM, VMEM, VMEM, ANY, VMEM, ANY],
        out_specs=[VMEM] * 5,
        out_shape=[
            jax.ShapeDtypeStruct((rows // 2, slots + rows), BF16),
            jax.ShapeDtypeStruct((rows // 2, slots), F32),
            jax.ShapeDtypeStruct((rows, depth), BF16),
            jax.ShapeDtypeStruct((factors.shape[0], rows), F32),
            pltpu.VMEM((slots, depth), BF16),
        ],
        scratch_shapes=[
            pltpu.VMEM((rows, depth), BF16),
            pltpu.VMEM(factors.shape, F32),
            pltpu.SemaphoreType.DMA,
            pltpu.SemaphoreType.DMA((LOADS,)),
        ],
        compiler_params=PARAMS,
        cost_estimate=estimate(slots, depth, rows),
        name="project_first",
    )(scalars, packed_other, packed_own, in_hbm(factors), in_vmem(near), in_hbm(samples))


def project_second(scalars, rows, near):
    slots, depth = near.shape
    half = rows.shape[0] // 2
    return pl.pallas_call(
        functools.partial(second_kernel, pattern=1 if ALTERNATE else 0),
        in_specs=[SMEM, VMEM, VMEM],
        out_specs=[VMEM] * 2,
        out_shape=[
            jax.ShapeDtypeStruct((half, slots), BF16),
            jax.ShapeDtypeStruct((half, slots), F32),
        ],
        scratch_shapes=[pltpu.VMEM(rows.shape, BF16)],
        compiler_params=PARAMS,
        cost_estimate=estimate(slots, depth, rows.shape[0]),
        name="project_second",
    )(scalars, rows, in_vmem(near))


def cross_kernel(scalars, mine, other, near, *refs, pattern, sides, add, tile):
    terms, refs = (refs[0] if add else None), refs[add:]
    outs, rows = refs[:-1], refs[-1]
    block = mine.shape[0] // 2
    half = 2 * block
    for i, piece in enumerate((other[:block], other[block:], mine[:block], mine[block:])):
        at = pl.multiple_of(scalars[4 * pattern + i] * block, block)
        rows[pl.ds(at, block), :] = piece
    width = outs[0].shape[1]
    first = sides[0] * half
    used = slice(first, first + len(sides) * half)

    @pl.loop(0, width // tile)
    def _(i):
        here = pl.ds(pl.multiple_of(i * tile, tile), tile)
        there = pl.ds(pl.multiple_of(width + i * tile, tile), tile)
        left, right = (
            jnp.dot(rows[used, :], near[:, at], preferred_element_type=F32) for at in (here, there)
        )
        for place, out in enumerate(outs):
            for chip in range(CHIPS):
                at = place * half + 8 * chip
                to = slice(16 * chip, 16 * chip + 16)
                value = jnp.concatenate([left[at : at + 8], right[at : at + 8]], 0)
                if add:
                    value = value + terms[to, here]
                out[to, here] = value.astype(out.dtype)


def cross(scalars, pieces, near, pattern, sides, out_type, term=None, tile=1024):
    slots, depth = near.shape
    rows = 2 * pieces[0].shape[0]
    add = term is not None
    out = jax.ShapeDtypeStruct((rows, depth // 2), out_type)
    return pl.pallas_call(
        functools.partial(cross_kernel, pattern=pattern, sides=sides, add=add, tile=tile),
        in_specs=[SMEM] + [VMEM] * (3 + add),
        out_specs=[VMEM] * len(sides),
        out_shape=[out] * len(sides),
        scratch_shapes=[pltpu.VMEM((rows, slots), BF16)],
        compiler_params=PARAMS,
        cost_estimate=estimate(slots, depth, rows),
        name="cross",
    )(scalars, *pieces, in_vmem(near), *([term] if add else []))


def split_dot(left, right, dims):
    both = lax.dot_general(
        jnp.concatenate(parts_of(left), 0), right, (dims, ((), ())), preferred_element_type=F32
    )
    return both[: left.shape[0]] + both[left.shape[0] :]


def on_device(samples, factors, weights, counts):
    owned, depth = factors.shape
    all_rows = weights.shape[0]
    half_rows = all_rows // 2
    block = all_rows // 4
    slots = samples.shape[0] // PARTS
    dp = lax.axis_index("dp")
    y = lax.axis_index("feat")
    core = lax.rem(dp, 2)
    chip = dp // 2
    first = jnp.where(core == 0, y ^ 1, 3 - y)
    second = jnp.where(core == 0, 3 - y, y ^ 1)
    across = lax.rem(y + 2, 4)
    order = []
    for one, two in ((first, second), (second, first)):
        for pair in ((one, across), (y, two)):
            order += [jnp.minimum(*pair), jnp.maximum(*pair)]
    scalars = jnp.stack(order + [counts[dp]]).astype(jnp.int32)
    total = jnp.sum(counts).astype(F32)
    by_core = weights.reshape(CHIPS, 2, owned).transpose(1, 0, 2).reshape(2, half_rows)
    weight_own = lax.dynamic_slice(by_core, (core, 0), (1, half_rows))[0]
    weight_other = lax.dynamic_slice(by_core, (1 - core, 0), (1, half_rows))[0]
    weight = jnp.concatenate([weight_other, weight_own])
    scales = []
    for part in range(PARTS):
        pattern = part if ALTERNATE else 0
        starts = [order[4 * pattern + i] * block for i in (2, 3)]
        scales.append(
            jnp.concatenate([lax.dynamic_slice(weight, (start,), (block,)) for start in starts])
        )
    weight_mine = lax.dynamic_slice(weight_own, (chip * owned,), (owned,))
    pairs = weight_mine[:, None] * weight[None, :]
    mine = lax.broadcasted_iota(jnp.int32, pairs.shape, 0) + half_rows + chip * owned
    here = (lax.broadcasted_iota(jnp.int32, pairs.shape, 1) == mine).astype(F32)
    factor = jnp.full((1, 1), 8.0, F32) / total[None, None]

    packed_own = plane_exchange(spread(factors))
    packed_own, scalars, scales, pairs, here, factor, samples = lax.optimization_barrier(
        (packed_own, scalars, scales, pairs, here, factor, samples)
    )
    near0 = load(samples)
    packed_other = core_swap(packed_own)

    sent0, kept0, rows, gram, near1 = project_first(
        scalars, packed_other, packed_own, factors, near0, samples
    )
    sent1, kept1 = project_second(scalars, rows, near1)

    def cubes_of(part, sent, kept, gram=None):
        pattern = part if ALTERNATE else 0
        one, two = PARTNERS[::-1] if pattern else PARTNERS
        got = feat_swap(sent, one)
        if gram is not None:
            gram = gram + gram_of(got[:16, slots:])
            got = got[:, :slots]
        value = kept + got.astype(F32)
        message = value.astype(BF16)
        if gram is not None:
            extra = jnp.pad(gram_message(gram), ((0, value.shape[0] - 16), (0, 0)))
            message = jnp.concatenate([message, extra], 1)
        passed = feat_swap(message, two)
        if gram is not None:
            gram = gram + gram_of(passed[:16, slots:])
            passed = passed[:, :slots]
        value = value + passed.astype(F32)
        cubes = (scales[part][:, None] * value**3).astype(BF16)
        return [cubes, feat_swap(cubes, one)], gram

    pieces0, gram = cubes_of(0, sent0, kept0, gram)
    pieces1, _ = cubes_of(1, sent1, kept1)
    other0, own0 = cross(scalars, pieces0, near0, 0, (0, 1), F32)
    pattern = 1 if ALTERNATE else 0
    (other1,) = cross(scalars, pieces1, near1, pattern, (0,), BF16, other0)
    (own1,) = cross(scalars, pieces1, near1, pattern, (1,), F32, own0)
    total_own = (own1 + core_swap(other1).astype(F32)).astype(BF16)
    blocks = plane_exchange(total_own).reshape(CHIPS, 2 * owned, depth // 2)
    cross_term = jnp.sum(blocks.astype(F32), axis=0)
    cross_term = jnp.concatenate([cross_term[:owned], cross_term[owned:]], 1)

    coupling = pairs * gram**3
    diagonal = jnp.sum(here * coupling, 1, keepdims=True)
    model_term = split_dot(coupling, rows, ((1,), (0,))) + diagonal * (
        factors - factors.astype(BF16).astype(F32)
    )
    return 8.0 * model_term - factor * cross_term


def solution(mesh):
    in_specs = (P("dp", "feat"), P("dp", "feat"), P(), P())
    out_specs = P("dp", "feat")
    return jax.shard_map(
        on_device, mesh=mesh, in_specs=in_specs, out_specs=out_specs, check_vma=False
    )
```

```python
import functools

import jax
import jax.numpy as jnp
from jax import lax
from jax.experimental import pallas as pl
from jax.experimental.pallas import tpu as pltpu
from jax.sharding import PartitionSpec as P

BF16 = jnp.bfloat16
F32 = jnp.float32
N_DP = 32
N_FEAT = 4
CHIPS = N_DP // 2
SIZES = (1664, 1408)
GRAM_PART = 0
LANES = 128
PARTS = len(SIZES)
LOADS = 2
PLANES = [[2 * chip + core for chip in range(CHIPS)] for core in range(2)]
VMEM = pl.BlockSpec(memory_space=pltpu.VMEM)
SMEM = pl.BlockSpec(memory_space=pltpu.SMEM)
ANY = pl.BlockSpec(memory_space=pl.ANY)
PARAMS = pltpu.CompilerParams(vmem_limit_bytes=8 << 20)


def in_hbm(array):
    return pltpu.with_memory_space_constraint(array, pltpu.HBM)


def in_vmem(array):
    return pltpu.with_memory_space_constraint(array, pltpu.VMEM)


def partner_first(core, y):
    return y ^ 1 if core == 0 else 3 - y


def partner_second(core, y):
    return 3 - y if core == 0 else y ^ 1


PARTNERS = (partner_first, partner_second)


def feat_swap(x, partner):
    pairs = []
    for dp in range(N_DP):
        for y in range(N_FEAT):
            pairs.append((dp * N_FEAT + y, dp * N_FEAT + partner(dp % 2, y)))
    return lax.ppermute(x, ("dp", "feat"), pairs)


def core_swap(x):
    return lax.ppermute(x, "dp", [(i, i ^ 1) for i in range(N_DP)])


def plane_exchange(x):
    return lax.all_to_all(x, "dp", 0, 0, axis_index_groups=PLANES, tiled=True)


def spread_kernel(factors, out):
    width = out.shape[1]
    block = jnp.concatenate([factors[:, :width], factors[:, width:]], 0).astype(BF16)
    for chip in range(CHIPS):
        out[pl.ds(16 * chip, 16), :] = block


def spread(factors):
    return pl.pallas_call(
        spread_kernel,
        in_specs=[VMEM],
        out_specs=VMEM,
        out_shape=pltpu.VMEM((16 * CHIPS, factors.shape[1] // 2), BF16),
        compiler_params=PARAMS,
        name="spread",
    )(in_hbm(factors))


def unpack(packed, out, top):
    for pair in range(CHIPS // 2):
        block = packed[pl.ds(32 * pair, 32), :].astype(F32)
        upper = jnp.concatenate([block[:8], block[8:16]], 1)
        lower = jnp.concatenate([block[16:24], block[24:]], 1)
        out[pl.ds(top + 16 * pair, 16), :] = jnp.concatenate([upper, lower], 0).astype(BF16)


def parts_of(value):
    high = value.astype(BF16)
    return high, (value - high.astype(F32)).astype(BF16)


def gram_message(gram):
    return jnp.concatenate([part.astype(F32) for part in parts_of(gram)], 0).astype(BF16)


def gram_of(message):
    value = message.astype(F32)
    return value[:8] + value[8:16]


def folded(value):
    return jnp.concatenate([value[:, :LANES], value[:, LANES:]], 0)


def gram_from(message):
    value = message.astype(F32)
    return jnp.concatenate([gram_of(value[:16]), gram_of(value[16:32])], 1)


def start_of(part):
    return sum(SIZES[:part])


def fetch(samples, near, sems, part):
    rows = SIZES[part] // LOADS
    copies = []
    for i in range(LOADS):
        here = pl.ds(i * rows, rows)
        there = pl.ds(start_of(part) + i * rows, rows)
        copies.append(pltpu.make_async_copy(samples.at[there, :], near.at[here, :], sems.at[i]))
        copies[-1].start()
    return copies


def load_kernel(packed, factors, samples, near, rows, left, gram, mine, sem, sems):
    first = pltpu.make_async_copy(factors, mine, sem)
    first.start()
    copies = fetch(samples, near, sems, 0)
    unpack(packed, rows, 0)
    first.wait()
    left[...] = gram_message(mine[...])
    gram[...] = gram_of(nt_dot(left[...], rows[...]))
    for copy in copies:
        copy.wait()


def load(packed, factors, samples):
    depth = samples.shape[1]
    count = packed.shape[0] // 2
    return pl.pallas_call(
        load_kernel,
        in_specs=[VMEM, ANY, ANY],
        out_specs=[VMEM] * 4,
        out_shape=[
            pltpu.VMEM((SIZES[0], depth), BF16),
            jax.ShapeDtypeStruct((count, depth), BF16),
            jax.ShapeDtypeStruct((2 * factors.shape[0], depth), BF16),
            jax.ShapeDtypeStruct((factors.shape[0], count), F32),
        ],
        scratch_shapes=[
            pltpu.VMEM(factors.shape, F32),
            pltpu.SemaphoreType.DMA,
            pltpu.SemaphoreType.DMA((LOADS,)),
        ],
        compiler_params=PARAMS,
        cost_estimate=pl.CostEstimate(
            flops=0, bytes_accessed=4 * SIZES[0] * depth, transcendentals=0
        ),
        name="load",
    )(packed, in_hbm(factors), in_hbm(samples))


def nt_dot(left, right):
    return lax.dot_general(left, right, (((1,), (1,)), ((), ())), preferred_element_type=F32)


def project_part(scalars, other, own, near, sent, kept, scratch, part):
    half, slots = kept.shape
    block = half // 2
    for i in range(4):
        quarter = scalars[i]
        at = pl.ds(pl.multiple_of(lax.rem(quarter, 2) * block, block), block)
        to = slice(i * block, (i + 1) * block)
        for side, ref in enumerate((other, own)):

            @pl.when(quarter // 2 == side)
            def _():
                scratch[to, :] = ref[at, :]

    value = nt_dot(scratch[...], near[...])
    slot = start_of(part) + lax.broadcasted_iota(jnp.int32, (1, slots), 1)
    value = jnp.where(slot < scalars[4], value, 0.0)
    sent[:, :slots] = value[:half].astype(BF16)
    kept[...] = value[half:]


def put_gram(sent, gram):
    slots = sent.shape[1] - LANES
    message = folded(gram_message(gram[...]).astype(F32)).astype(BF16)
    sent[:32, slots:] = message
    sent[32:, slots:] = jnp.zeros((sent.shape[0] - 32, LANES), BF16)


def first_kernel(scalars, packed, own, left, gram_own, near, samples, sent, kept, other, gram, later, scratch, sems):
    copies = fetch(samples, later, sems, 1)
    unpack(packed, other, 0)
    project_part(scalars, other, own, near, sent, kept, scratch, 0)
    gram[...] = jnp.concatenate([gram_of(nt_dot(left[...], other[...])), gram_own[...]], 1)
    if GRAM_PART == 0:
        put_gram(sent, gram)
    for copy in copies:
        copy.wait()


def project_first(scalars, packed, own, left, gram_own, near, samples):
    slots, depth = near.shape
    count = 2 * own.shape[0]
    return pl.pallas_call(
        first_kernel,
        in_specs=[SMEM] + [VMEM] * 5 + [ANY],
        out_specs=[VMEM] * 5,
        out_shape=[
            jax.ShapeDtypeStruct((count // 2, slots + LANES * (GRAM_PART == 0)), BF16),
            jax.ShapeDtypeStruct((count // 2, slots), F32),
            jax.ShapeDtypeStruct((count // 2, depth), BF16),
            jax.ShapeDtypeStruct((left.shape[0] // 2, count), F32),
            pltpu.VMEM((SIZES[1], depth), BF16),
        ],
        scratch_shapes=[
            pltpu.VMEM((count, depth), BF16),
            pltpu.SemaphoreType.DMA((LOADS,)),
        ],
        compiler_params=PARAMS,
        cost_estimate=estimate(slots, depth, count),
        name="project_first",
    )(scalars, packed, own, left, gram_own, in_vmem(near), in_hbm(samples))


def second_kernel(scalars, other, own, gram, near, sent, kept, scratch):
    project_part(scalars, other, own, near, sent, kept, scratch, 1)
    if GRAM_PART == 1:
        put_gram(sent, gram)


def project_second(scalars, other, own, gram, near):
    slots, depth = near.shape
    count = 2 * own.shape[0]
    return pl.pallas_call(
        second_kernel,
        in_specs=[SMEM] + [VMEM] * 4,
        out_specs=[VMEM] * 2,
        out_shape=[
            jax.ShapeDtypeStruct((count // 2, slots + LANES * (GRAM_PART == 1)), BF16),
            jax.ShapeDtypeStruct((count // 2, slots), F32),
        ],
        scratch_shapes=[pltpu.VMEM((count, depth), BF16)],
        compiler_params=PARAMS,
        cost_estimate=estimate(slots, depth, count),
        name="project_second",
    )(scalars, other, own, gram, in_vmem(near))


def estimate(slots, depth, rows):
    return pl.CostEstimate(
        flops=2 * slots * depth * rows, bytes_accessed=2 * slots * depth, transcendentals=0
    )


def model_kernel(pairs, here, gram, other, own, factors, out):
    value = pairs[...] * gram[...] * gram[...] * gram[...]
    diagonal = jnp.sum(here[...] * value, 1, keepdims=True)
    left = gram_message(value)
    half = other.shape[0]
    both = jnp.dot(left[:, :half], other[...], preferred_element_type=F32) + jnp.dot(
        left[:, half:], own[...], preferred_element_type=F32
    )
    rest = factors[...] - factors[...].astype(BF16).astype(F32)
    out[...] = 8.0 * (gram_of(both) + diagonal * rest)


def model(pairs, here, gram, other, own, factors):
    return pl.pallas_call(
        model_kernel,
        in_specs=[VMEM] * 6,
        out_specs=VMEM,
        out_shape=jax.ShapeDtypeStruct(factors.shape, F32),
        compiler_params=PARAMS,
        name="model",
    )(pairs, here, gram, other, own, factors)


def cross_kernel(scalars, mine, other, near, *refs, sides, add, tile):
    terms, refs = (refs[: len(sides)] if add else None), refs[add * len(sides) :]
    outs, rows = refs[:-1], refs[-1]
    block = mine.shape[0] // 2
    half = 2 * block
    for i, piece in enumerate((other[:block], other[block:], mine[:block], mine[block:])):
        at = pl.multiple_of(scalars[i] * block, block)
        rows[pl.ds(at, block), :] = piece
    width = outs[0].shape[1]
    first = sides[0] * half
    used = slice(first, first + len(sides) * half)

    @pl.loop(0, width // tile)
    def _(i):
        here = pl.ds(pl.multiple_of(i * tile, tile), tile)
        there = pl.ds(pl.multiple_of(width + i * tile, tile), tile)
        left, right = (
            jnp.dot(rows[used, :], near[:, at], preferred_element_type=F32) for at in (here, there)
        )
        for place, out in enumerate(outs):
            for chip in range(CHIPS):
                at = place * half + 8 * chip
                to = slice(16 * chip, 16 * chip + 16)
                value = jnp.concatenate([left[at : at + 8], right[at : at + 8]], 0)
                if add:
                    value = value + terms[place][to, here]
                out[to, here] = value.astype(out.dtype)


def cross(scalars, pieces, near, sides, out_type, terms=(), tile=512):
    slots, depth = near.shape
    rows = 2 * pieces[0].shape[0]
    out = jax.ShapeDtypeStruct((rows, depth // 2), out_type)
    return pl.pallas_call(
        functools.partial(cross_kernel, sides=sides, add=bool(terms), tile=tile),
        in_specs=[SMEM] + [VMEM] * (3 + len(terms)),
        out_specs=[VMEM] * len(sides),
        out_shape=[out] * len(sides),
        scratch_shapes=[pltpu.VMEM((rows, slots), BF16)],
        compiler_params=PARAMS,
        cost_estimate=estimate(slots, depth, rows),
        name="cross",
    )(scalars, *pieces, in_vmem(near), *terms)


def add_kernel(left, right, out):
    out[...] = (left[...] + right[...].astype(F32)).astype(BF16)


def add(left, right):
    return pl.pallas_call(
        add_kernel,
        in_specs=[VMEM, VMEM],
        out_specs=VMEM,
        out_shape=pltpu.VMEM(left.shape, BF16),
        compiler_params=PARAMS,
        name="add",
    )(left, right)


def on_device(samples, factors, weights, counts):
    owned, depth = factors.shape
    all_rows = weights.shape[0]
    half_rows = all_rows // 2
    block = all_rows // 4
    dp = lax.axis_index("dp")
    y = lax.axis_index("feat")
    core = lax.rem(dp, 2)
    chip = dp // 2
    first = jnp.where(core == 0, y ^ 1, 3 - y)
    second = jnp.where(core == 0, 3 - y, y ^ 1)
    across = lax.rem(y + 2, 4)
    order = []
    for pair in ((first, across), (y, second)):
        order += [jnp.minimum(*pair), jnp.maximum(*pair)]
    scalars = jnp.stack(order + [counts[dp]]).astype(jnp.int32)
    total = jnp.sum(counts).astype(F32)
    by_core = weights.reshape(CHIPS, 2, owned).transpose(1, 0, 2).reshape(2, half_rows)
    weight_own = lax.dynamic_slice(by_core, (core, 0), (1, half_rows))[0]
    weight_other = lax.dynamic_slice(by_core, (1 - core, 0), (1, half_rows))[0]
    weight = jnp.concatenate([weight_other, weight_own])
    scale = jnp.concatenate(
        [lax.dynamic_slice(weight, (order[i] * block,), (block,)) for i in (2, 3)]
    )
    scales = [scale] * PARTS
    weight_mine = lax.dynamic_slice(weight_own, (chip * owned,), (owned,))
    pairs = weight_mine[:, None] * weight[None, :]
    mine = lax.broadcasted_iota(jnp.int32, pairs.shape, 0) + half_rows + chip * owned
    here = (lax.broadcasted_iota(jnp.int32, pairs.shape, 1) == mine).astype(F32)
    factor = jnp.full((1, 1), 8.0, F32) / total[None, None]

    packed_own = plane_exchange(spread(factors))
    packed_own, scalars, scales, pairs, here, factor, samples = lax.optimization_barrier(
        (packed_own, scalars, scales, pairs, here, factor, samples)
    )
    near0, own, left, gram_own = load(packed_own, factors, samples)
    packed_other = core_swap(packed_own)
    sent0, kept0, other, gram, near1 = project_first(
        scalars, packed_other, own, left, gram_own, near0, samples
    )
    sent1, kept1 = project_second(scalars, other, own, gram, near1)
    nears = (near0, near1)

    pieces = []
    for part, (sent, kept) in enumerate(((sent0, kept0), (sent1, kept1))):
        slots = kept.shape[1]
        carries = part == GRAM_PART
        with jax.named_scope(f"halves{part}"):
            got = feat_swap(sent, partner_first)
        value = kept + got[:, :slots].astype(F32)
        message = value.astype(BF16)
        if carries:
            gram = gram + gram_from(got[:32, slots:])
            high = lax.reduce_precision(gram, 8, 7)
            extra = folded(jnp.concatenate([high, gram - high], 0)).astype(BF16)
            extra = jnp.pad(extra, ((0, kept.shape[0] - 32), (0, 0)))
            message = jnp.concatenate([message, extra], 1)
        with jax.named_scope(f"sums{part}"):
            passed = feat_swap(message, partner_second)
        if carries:
            gram = gram + gram_from(passed[:32, slots:])
        value = value + passed[:, :slots].astype(F32)
        cubes = (scales[part][:, None] * value**3).astype(BF16)
        with jax.named_scope(f"cubes{part}"):
            pieces.append((cubes, feat_swap(cubes, partner_first)))

    terms = ()
    for part in range(PARTS - 1):
        terms = cross(scalars, pieces[part], nears[part], (0, 1), F32, terms)
    (sum_other,) = cross(scalars, pieces[-1], nears[-1], (0,), BF16, terms[:1])
    (sum_own,) = cross(scalars, pieces[-1], nears[-1], (1,), F32, terms[1:])
    total_own = add(sum_own, core_swap(sum_other))
    model_term = model(pairs, here, gram, other, own, factors)
    model_term, total_own = lax.optimization_barrier((model_term, total_own))
    blocks = plane_exchange(total_own).reshape(CHIPS, 2 * owned, depth // 2)
    cross_term = jnp.sum(blocks.astype(F32), axis=0)
    cross_term = jnp.concatenate([cross_term[:owned], cross_term[owned:]], 1)

    return model_term - factor * cross_term


def solution(mesh):
    in_specs = (P("dp", "feat"), P("dp", "feat"), P(), P())
    out_specs = P("dp", "feat")
    return jax.shard_map(
        on_device, mesh=mesh, in_specs=in_specs, out_specs=out_specs, check_vma=False
    )
```

```python
import functools

import jax
import jax.numpy as jnp
from jax import lax
from jax.experimental import pallas as pl
from jax.experimental.pallas import tpu as pltpu
from jax.sharding import PartitionSpec as P

BF16 = jnp.bfloat16
F32 = jnp.float32
N_DP = 32
N_FEAT = 4
CHIPS = N_DP // 2
SIZES = (1664, 1408)
GRAM_PART = 0
LANES = 128
PARTS = len(SIZES)
LOADS = 2
PLANES = [[2 * chip + core for chip in range(CHIPS)] for core in range(2)]
VMEM = pl.BlockSpec(memory_space=pltpu.VMEM)
SMEM = pl.BlockSpec(memory_space=pltpu.SMEM)
ANY = pl.BlockSpec(memory_space=pl.ANY)
PARAMS = pltpu.CompilerParams(vmem_limit_bytes=8 << 20)


def in_hbm(array):
    return pltpu.with_memory_space_constraint(array, pltpu.HBM)


def in_vmem(array):
    return pltpu.with_memory_space_constraint(array, pltpu.VMEM)


def partner_first(core, y):
    return y ^ 1 if core == 0 else 3 - y


def partner_second(core, y):
    return 3 - y if core == 0 else y ^ 1


PARTNERS = (partner_first, partner_second)


def feat_swap(x, partner):
    pairs = []
    for dp in range(N_DP):
        for y in range(N_FEAT):
            pairs.append((dp * N_FEAT + y, dp * N_FEAT + partner(dp % 2, y)))
    return lax.ppermute(x, ("dp", "feat"), pairs)


def core_swap(x):
    return lax.ppermute(x, "dp", [(i, i ^ 1) for i in range(N_DP)])


def plane_exchange(x):
    return lax.all_to_all(x, "dp", 0, 0, axis_index_groups=PLANES, tiled=True)


def spread_kernel(factors, out):
    width = out.shape[1]
    block = jnp.concatenate([factors[:, :width], factors[:, width:]], 0).astype(BF16)
    for chip in range(CHIPS):
        out[pl.ds(16 * chip, 16), :] = block


def spread(factors):
    return pl.pallas_call(
        spread_kernel,
        in_specs=[VMEM],
        out_specs=VMEM,
        out_shape=pltpu.VMEM((16 * CHIPS, factors.shape[1] // 2), BF16),
        compiler_params=PARAMS,
        name="spread",
    )(in_hbm(factors))


def unpack(packed, out, top):
    for pair in range(CHIPS // 2):
        block = packed[pl.ds(32 * pair, 32), :].astype(F32)
        upper = jnp.concatenate([block[:8], block[8:16]], 1)
        lower = jnp.concatenate([block[16:24], block[24:]], 1)
        out[pl.ds(top + 16 * pair, 16), :] = jnp.concatenate([upper, lower], 0).astype(BF16)


def parts_of(value):
    high = value.astype(BF16)
    return high, (value - high.astype(F32)).astype(BF16)


def gram_message(gram):
    return jnp.concatenate([part.astype(F32) for part in parts_of(gram)], 0).astype(BF16)


def gram_of(message):
    value = message.astype(F32)
    return value[:8] + value[8:16]


def folded(value):
    return jnp.concatenate([value[:, :LANES], value[:, LANES:]], 0)


def gram_from(message):
    value = message.astype(F32)
    return jnp.concatenate([gram_of(value[:16]), gram_of(value[16:32])], 1)


def start_of(part):
    return sum(SIZES[:part])


def fetch(samples, near, sems, part):
    rows = SIZES[part] // LOADS
    copies = []
    for i in range(LOADS):
        here = pl.ds(i * rows, rows)
        there = pl.ds(start_of(part) + i * rows, rows)
        copies.append(pltpu.make_async_copy(samples.at[there, :], near.at[here, :], sems.at[i]))
        copies[-1].start()
    return copies


def place_of():
    dp = lax.axis_index("dp")
    return dp, lax.axis_index("feat"), dp & 1, dp >> 1


def order_of():
    _, y, core, _ = place_of()
    first = jnp.where(core == 0, y ^ 1, 3 - y)
    second = jnp.where(core == 0, 3 - y, y ^ 1)
    order = []
    for pair in ((first, y ^ 2), (y, second)):
        order += [jnp.minimum(*pair), jnp.maximum(*pair)]
    return order


def chosen(weights, numbers):
    lanes = lax.broadcasted_iota(jnp.int32, (numbers.shape[0], weights.shape[1]), 1)
    return jnp.sum(jnp.where(lanes == numbers, weights, 0.0), 1, keepdims=True)


def number(place, count, core):
    half = count // 2
    inside = place & (half - 1)
    side = jnp.where(place < half, 1 - core, core)
    return (inside >> 3) * 16 + side * 8 + (inside & 7)


def load_kernel(counts, weights, packed, factors, samples, *refs):
    near, rows, left, gram, scale, *masks, mine, row, numbers, sem, small, sems = refs
    first = pltpu.make_async_copy(factors, mine, sem)
    first.start()
    others = [
        pltpu.make_async_copy(weights, row, small.at[0]),
        pltpu.make_async_copy(counts, numbers, small.at[1]),
    ]
    for copy in others:
        copy.start()
    copies = fetch(samples, near, sems, 0)
    unpack(packed, rows, 0)
    first.wait()
    left[...] = gram_message(mine[...])
    gram[...] = gram_of(nt_dot(left[...], rows[...]))
    for copy in others:
        copy.wait()
    order = order_of()
    dp, _, core, _ = place_of()
    for part, mask in enumerate(masks):
        slot = start_of(part) + lax.broadcasted_iota(jnp.int32, mask.shape, 1)
        mask[...] = jnp.where(slot < numbers[dp], 1.0, 0.0)
    half = scale.shape[0]
    block = half // 2
    step = lax.broadcasted_iota(jnp.int32, (half, 1), 0)
    at = jnp.where(step < block, order[2] * block + step, (order[3] - 1) * block + step)
    scale[...] = chosen(row[...].reshape(1, 2 * half), number(at, 2 * half, core))
    for copy in copies:
        copy.wait()


def load(counts, weights, packed, factors, samples):
    depth = samples.shape[1]
    owned = factors.shape[0]
    half = packed.shape[0] // 2
    return pl.pallas_call(
        load_kernel,
        in_specs=[ANY, ANY, VMEM, ANY, ANY],
        out_specs=[VMEM] * (5 + PARTS),
        out_shape=[
            pltpu.VMEM((SIZES[0], depth), BF16),
            jax.ShapeDtypeStruct((half, depth), BF16),
            jax.ShapeDtypeStruct((2 * owned, depth), BF16),
            jax.ShapeDtypeStruct((owned, half), F32),
            jax.ShapeDtypeStruct((half, 1), F32),
        ]
        + [jax.ShapeDtypeStruct((1, size), F32) for size in SIZES],
        scratch_shapes=[
            pltpu.VMEM(factors.shape, F32),
            pltpu.VMEM(weights.shape, F32),
            pltpu.SMEM(counts.shape, jnp.int32),
            pltpu.SemaphoreType.DMA,
            pltpu.SemaphoreType.DMA((2,)),
            pltpu.SemaphoreType.DMA((LOADS,)),
        ],
        compiler_params=PARAMS,
        cost_estimate=pl.CostEstimate(
            flops=0, bytes_accessed=4 * SIZES[0] * depth, transcendentals=0
        ),
        name="load",
    )(in_hbm(counts), in_hbm(weights), packed, in_hbm(factors), in_hbm(samples))


def cube_kernel(scale, value, passed, out):
    slots = value.shape[1]
    total = value[...] + passed[:, :slots].astype(F32)
    out[...] = (scale[...] * (total * total * total)).astype(BF16)


def cube(scale, value, passed):
    return pl.pallas_call(
        cube_kernel,
        in_specs=[VMEM] * 3,
        out_specs=VMEM,
        out_shape=jax.ShapeDtypeStruct(value.shape, BF16),
        compiler_params=PARAMS,
        cost_estimate=pl.CostEstimate(
            flops=4 * value.size, bytes_accessed=8 * value.size, transcendentals=0
        ),
        name="cube",
    )(scale, value, passed)


def nt_dot(left, right):
    return lax.dot_general(left, right, (((1,), (1,)), ((), ())), preferred_element_type=F32)


def project_part(mask, other, own, near, sent, kept, scratch):
    half, slots = kept.shape
    block = half // 2
    for i, quarter in enumerate(order_of()):
        at = pl.ds(pl.multiple_of(lax.rem(quarter, 2) * block, block), block)
        to = slice(i * block, (i + 1) * block)
        for side, ref in enumerate((other, own)):

            @pl.when(quarter // 2 == side)
            def _():
                scratch[to, :] = ref[at, :]

    value = nt_dot(scratch[...], near[...])
    value = value * mask[...]
    sent[:, :slots] = value[:half].astype(BF16)
    kept[...] = value[half:]


def put_gram(sent, gram):
    slots = sent.shape[1] - LANES
    message = folded(gram_message(gram[...]).astype(F32)).astype(BF16)
    sent[:32, slots:] = message
    sent[32:, slots:] = jnp.zeros((sent.shape[0] - 32, LANES), BF16)


def first_kernel(mask, packed, own, left, gram_own, near, samples, sent, kept, other, gram, later, scratch, sems):
    copies = fetch(samples, later, sems, 1)
    unpack(packed, other, 0)
    project_part(mask, other, own, near, sent, kept, scratch)
    gram[...] = jnp.concatenate([gram_of(nt_dot(left[...], other[...])), gram_own[...]], 1)
    if GRAM_PART == 0:
        put_gram(sent, gram)
    for copy in copies:
        copy.wait()


def project_first(mask, packed, own, left, gram_own, near, samples):
    slots, depth = near.shape
    count = 2 * own.shape[0]
    return pl.pallas_call(
        first_kernel,
        in_specs=[VMEM] * 6 + [ANY],
        out_specs=[VMEM] * 5,
        out_shape=[
            jax.ShapeDtypeStruct((count // 2, slots + LANES * (GRAM_PART == 0)), BF16),
            jax.ShapeDtypeStruct((count // 2, slots), F32),
            jax.ShapeDtypeStruct((count // 2, depth), BF16),
            jax.ShapeDtypeStruct((left.shape[0] // 2, count), F32),
            pltpu.VMEM((SIZES[1], depth), BF16),
        ],
        scratch_shapes=[
            pltpu.VMEM((count, depth), BF16),
            pltpu.SemaphoreType.DMA((LOADS,)),
        ],
        compiler_params=PARAMS,
        cost_estimate=estimate(slots, depth, count),
        name="project_first",
    )(mask, packed, own, left, gram_own, in_vmem(near), in_hbm(samples))


def second_kernel(mask, other, own, gram, near, sent, kept, scratch):
    project_part(mask, other, own, near, sent, kept, scratch)
    if GRAM_PART == 1:
        put_gram(sent, gram)


def project_second(mask, other, own, gram, near):
    slots, depth = near.shape
    count = 2 * own.shape[0]
    return pl.pallas_call(
        second_kernel,
        in_specs=[VMEM] * 5,
        out_specs=[VMEM] * 2,
        out_shape=[
            jax.ShapeDtypeStruct((count // 2, slots + LANES * (GRAM_PART == 1)), BF16),
            jax.ShapeDtypeStruct((count // 2, slots), F32),
        ],
        scratch_shapes=[pltpu.VMEM((count, depth), BF16)],
        compiler_params=PARAMS,
        cost_estimate=estimate(slots, depth, count),
        name="project_second",
    )(mask, other, own, gram, in_vmem(near))


def estimate(slots, depth, rows):
    return pl.CostEstimate(
        flops=2 * slots * depth * rows, bytes_accessed=2 * slots * depth, transcendentals=0
    )


def model_kernel(counts, weights, gram, other, own, factors, out, inverse):
    _, _, core, chip = place_of()
    owned, count = gram.shape
    half = count // 2
    row = weights[...].reshape(1, count)
    column = chosen(row, number(lax.broadcasted_iota(jnp.int32, (count, 1), 0), count, core))
    down = lax.broadcasted_iota(jnp.int32, (count, count), 0)
    along = lax.broadcasted_iota(jnp.int32, (count, count), 1)
    weight = jnp.sum(jnp.where(down == along, column, 0.0), 0, keepdims=True)
    mine = half + chip * owned + lax.broadcasted_iota(jnp.int32, (owned, 1), 0)
    pairs = chosen(row, number(mine, count, core)) * weight
    value = pairs * gram[...] * gram[...] * gram[...]
    lanes = lax.broadcasted_iota(jnp.int32, (owned, count), 1)
    diagonal = jnp.sum(jnp.where(lanes == mine, value, 0.0), 1, keepdims=True)
    left = gram_message(value)
    both = jnp.dot(left[:, :half], other[...], preferred_element_type=F32) + jnp.dot(
        left[:, half:], own[...], preferred_element_type=F32
    )
    rest = factors[...] - factors[...].astype(BF16).astype(F32)
    out[...] = 8.0 * (gram_of(both) + diagonal * rest)
    total = counts[0]
    for i in range(1, N_DP):
        total = total + counts[i]
    inverse[...] = 8.0 / jnp.full(inverse.shape, total, jnp.int32).astype(F32)


def model(counts, weights, gram, other, own, factors):
    return pl.pallas_call(
        model_kernel,
        in_specs=[SMEM] + [VMEM] * 5,
        out_specs=[VMEM] * 2,
        out_shape=[
            jax.ShapeDtypeStruct(factors.shape, F32),
            jax.ShapeDtypeStruct((1, factors.shape[1]), F32),
        ],
        compiler_params=PARAMS,
        name="model",
    )(counts, weights, gram, other, own, factors)


def finish_kernel(blocks, model_term, inverse, out):
    rows, width = model_term.shape[0], blocks.shape[1]
    total = jnp.zeros((2 * rows, width), F32)
    for chip in range(CHIPS):
        total = total + blocks[pl.ds(16 * chip, 16), :].astype(F32)
    total = jnp.concatenate([total[:rows], total[rows:]], 1)
    out[...] = model_term[...] - inverse[...] * total


def finish(blocks, model_term, inverse):
    return pl.pallas_call(
        finish_kernel,
        in_specs=[VMEM] * 3,
        out_specs=VMEM,
        out_shape=jax.ShapeDtypeStruct(model_term.shape, F32),
        compiler_params=PARAMS,
        name="finish",
    )(blocks, model_term, inverse)


def cross_kernel(mine, other, near, *refs, sides, add, tile):
    terms, refs = (refs[: len(sides)] if add else None), refs[add * len(sides) :]
    outs, rows = refs[:-1], refs[-1]
    block = mine.shape[0] // 2
    half = 2 * block
    pieces = (other[:block], other[block:], mine[:block], mine[block:])
    for quarter, piece in zip(order_of(), pieces):
        at = pl.multiple_of(quarter * block, block)
        rows[pl.ds(at, block), :] = piece
    width = outs[0].shape[1]
    first = sides[0] * half
    used = slice(first, first + len(sides) * half)

    @pl.loop(0, width // tile)
    def _(i):
        here = pl.ds(pl.multiple_of(i * tile, tile), tile)
        there = pl.ds(pl.multiple_of(width + i * tile, tile), tile)
        left, right = (
            jnp.dot(rows[used, :], near[:, at], preferred_element_type=F32) for at in (here, there)
        )
        for place, out in enumerate(outs):
            for chip in range(CHIPS):
                at = place * half + 8 * chip
                to = slice(16 * chip, 16 * chip + 16)
                value = jnp.concatenate([left[at : at + 8], right[at : at + 8]], 0)
                if add:
                    value = value + terms[place][to, here]
                out[to, here] = value.astype(out.dtype)


def cross(pieces, near, sides, out_type, terms=(), tile=512):
    slots, depth = near.shape
    rows = 2 * pieces[0].shape[0]
    out = jax.ShapeDtypeStruct((rows, depth // 2), out_type)
    return pl.pallas_call(
        functools.partial(cross_kernel, sides=sides, add=bool(terms), tile=tile),
        in_specs=[VMEM] * (3 + len(terms)),
        out_specs=[VMEM] * len(sides),
        out_shape=[out] * len(sides),
        scratch_shapes=[pltpu.VMEM((rows, slots), BF16)],
        compiler_params=PARAMS,
        cost_estimate=estimate(slots, depth, rows),
        name="cross",
    )(*pieces, in_vmem(near), *terms)


def add_kernel(left, right, out):
    out[...] = (left[...] + right[...].astype(F32)).astype(BF16)


def add(left, right):
    return pl.pallas_call(
        add_kernel,
        in_specs=[VMEM, VMEM],
        out_specs=VMEM,
        out_shape=pltpu.VMEM(left.shape, BF16),
        compiler_params=PARAMS,
        name="add",
    )(left, right)


def on_device(samples, factors, weights, counts):
    owned, depth = factors.shape
    packed_own = plane_exchange(spread(factors))
    near0, own, left, gram_own, scale, mask0, mask1 = load(
        counts, weights, packed_own, factors, samples
    )
    packed_other = core_swap(packed_own)
    sent0, kept0, other, gram, near1 = project_first(
        mask0, packed_other, own, left, gram_own, near0, samples
    )
    sent1, kept1 = project_second(mask1, other, own, gram, near1)
    nears = (near0, near1)

    pieces = []
    for part, (sent, kept) in enumerate(((sent0, kept0), (sent1, kept1))):
        slots = kept.shape[1]
        carries = part == GRAM_PART
        with jax.named_scope(f"halves{part}"):
            got = feat_swap(sent, partner_first)
        value = kept + got[:, :slots].astype(F32)
        message = value.astype(BF16)
        if carries:
            gram = gram + gram_from(got[:32, slots:])
            high = lax.reduce_precision(gram, 8, 7)
            extra = folded(jnp.concatenate([high, gram - high], 0)).astype(BF16)
            extra = jnp.pad(extra, ((0, kept.shape[0] - 32), (0, 0)))
            message = jnp.concatenate([message, extra], 1)
        with jax.named_scope(f"sums{part}"):
            passed = feat_swap(message, partner_second)
        if carries:
            gram = gram + gram_from(passed[:32, slots:])
        if part == PARTS - 1:
            model_term, inverse = model(counts, weights, gram, other, own, factors)
            scale, model_term, inverse = lax.optimization_barrier((scale, model_term, inverse))
        cubes = cube(scale, value, passed)
        with jax.named_scope(f"cubes{part}"):
            pieces.append((cubes, feat_swap(cubes, partner_first)))

    terms = ()
    for part in range(PARTS - 1):
        terms = cross(pieces[part], nears[part], (0, 1), F32, terms)
    (sum_other,) = cross(pieces[-1], nears[-1], (0,), BF16, terms[:1])
    (sum_own,) = cross(pieces[-1], nears[-1], (1,), F32, terms[1:])
    total_own = add(sum_own, core_swap(sum_other))
    return finish(plane_exchange(total_own), model_term, inverse)


def solution(mesh):
    in_specs = (P("dp", "feat"), P("dp", "feat"), P(), P())
    out_specs = P("dp", "feat")
    return jax.shard_map(
        on_device, mesh=mesh, in_specs=in_specs, out_specs=out_specs, check_vma=False
    )
```

```python
import functools

import jax
import jax.numpy as jnp
from jax import lax
from jax.experimental import pallas as pl
from jax.experimental.pallas import tpu as pltpu
from jax.sharding import PartitionSpec as P

BF16 = jnp.bfloat16
F32 = jnp.float32
N_DP = 32
N_FEAT = 4
CHIPS = N_DP // 2
SIZES = (1664, 1408)
GRAM_PART = 0
LANES = 128
PARTS = len(SIZES)
LOADS = 1
PLANES = [[2 * chip + core for chip in range(CHIPS)] for core in range(2)]
VMEM = pl.BlockSpec(memory_space=pltpu.VMEM)
SMEM = pl.BlockSpec(memory_space=pltpu.SMEM)
ANY = pl.BlockSpec(memory_space=pl.ANY)
PARAMS = pltpu.CompilerParams(vmem_limit_bytes=8 << 20)


def in_hbm(array):
    return pltpu.with_memory_space_constraint(array, pltpu.HBM)


def in_vmem(array):
    return pltpu.with_memory_space_constraint(array, pltpu.VMEM)


def partner_first(core, y):
    return y ^ 1 if core == 0 else 3 - y


def partner_second(core, y):
    return 3 - y if core == 0 else y ^ 1


PARTNERS = (partner_first, partner_second)


def feat_swap(x, partner):
    pairs = []
    for dp in range(N_DP):
        for y in range(N_FEAT):
            pairs.append((dp * N_FEAT + y, dp * N_FEAT + partner(dp % 2, y)))
    return lax.ppermute(x, ("dp", "feat"), pairs)


def core_swap(x):
    return lax.ppermute(x, "dp", [(i, i ^ 1) for i in range(N_DP)])


def plane_exchange(x):
    return lax.all_to_all(x, "dp", 0, 0, axis_index_groups=PLANES, tiled=True)


def spread_kernel(factors, out):
    width = out.shape[1]
    block = jnp.concatenate([factors[:, :width], factors[:, width:]], 0).astype(BF16)
    for chip in range(CHIPS):
        out[pl.ds(16 * chip, 16), :] = block


def spread(factors):
    return pl.pallas_call(
        spread_kernel,
        in_specs=[VMEM],
        out_specs=VMEM,
        out_shape=pltpu.VMEM((16 * CHIPS, factors.shape[1] // 2), BF16),
        compiler_params=PARAMS,
        name="spread",
    )(in_hbm(factors))


def unpack(packed, out, top):
    for pair in range(CHIPS // 2):
        block = packed[pl.ds(32 * pair, 32), :].astype(F32)
        upper = jnp.concatenate([block[:8], block[8:16]], 1)
        lower = jnp.concatenate([block[16:24], block[24:]], 1)
        out[pl.ds(top + 16 * pair, 16), :] = jnp.concatenate([upper, lower], 0).astype(BF16)


def parts_of(value):
    high = value.astype(BF16)
    return high, (value - high.astype(F32)).astype(BF16)


def gram_message(gram):
    return jnp.concatenate([part.astype(F32) for part in parts_of(gram)], 0).astype(BF16)


def gram_of(message):
    value = message.astype(F32)
    return value[:8] + value[8:16]


def folded(value):
    return jnp.concatenate([value[:, :LANES], value[:, LANES:]], 0)


def gram_from(message):
    value = message.astype(F32)
    return jnp.concatenate([gram_of(value[:16]), gram_of(value[16:32])], 1)


def start_of(part):
    return sum(SIZES[:part])


def fetch(samples, near, sems, part):
    rows = SIZES[part] // LOADS
    copies = []
    for i in range(LOADS):
        here = pl.ds(i * rows, rows)
        there = pl.ds(start_of(part) + i * rows, rows)
        copies.append(pltpu.make_async_copy(samples.at[there, :], near.at[here, :], sems.at[i]))
        copies[-1].start()
    return copies


def place_of():
    dp = lax.axis_index("dp")
    return dp, lax.axis_index("feat"), dp & 1, dp >> 1


def order_of(core=None):
    _, y, mine, _ = place_of()
    core = mine if core is None else core
    first = jnp.where(core == 0, y ^ 1, 3 - y)
    second = jnp.where(core == 0, 3 - y, y ^ 1)
    order = []
    for pair in ((first, y ^ 2), (y, second)):
        order += [jnp.minimum(*pair), jnp.maximum(*pair)]
    return order


def chosen(weights, numbers):
    lanes = lax.broadcasted_iota(jnp.int32, (numbers.shape[0], weights.shape[1]), 1)
    return jnp.sum(jnp.where(lanes == numbers, weights, 0.0), 1, keepdims=True)


def number(place, count, core):
    half = count // 2
    inside = place & (half - 1)
    side = jnp.where(place < half, 1 - core, core)
    return (inside >> 3) * 16 + side * 8 + (inside & 7)


def load_kernel(counts, weights, packed, factors, samples, *refs):
    near, rows, left, gram, scale, *masks, mine, row, numbers, sem, small, sems = refs
    first = pltpu.make_async_copy(factors, mine, sem)
    first.start()
    others = [
        pltpu.make_async_copy(weights, row, small.at[0]),
        pltpu.make_async_copy(counts, numbers, small.at[1]),
    ]
    for copy in others:
        copy.start()
    copies = fetch(samples, near, sems, 0)
    unpack(packed, rows, 0)
    first.wait()
    left[...] = gram_message(mine[...])
    gram[...] = gram_of(nt_dot(left[...], rows[...]))
    for copy in others:
        copy.wait()
    order = order_of()
    dp, _, core, _ = place_of()
    for part, mask in enumerate(masks):
        slot = start_of(part) + lax.broadcasted_iota(jnp.int32, mask.shape, 1)
        mask[...] = jnp.where(slot < numbers[dp], 1.0, 0.0)
    half = scale.shape[0]
    block = half // 2
    step = lax.broadcasted_iota(jnp.int32, (half, 1), 0)
    tops = [(quarter & 1) * half + (quarter >> 1) * block for quarter in order[2:]]
    at = jnp.where(step < block, tops[0] + step, tops[1] + step - block)
    scale[...] = chosen(row[...].reshape(1, 2 * half), number(at, 2 * half, core))
    for copy in copies:
        copy.wait()


def load(counts, weights, packed, factors, samples):
    depth = samples.shape[1]
    owned = factors.shape[0]
    half = packed.shape[0] // 2
    return pl.pallas_call(
        load_kernel,
        in_specs=[ANY, ANY, VMEM, ANY, ANY],
        out_specs=[VMEM] * (5 + PARTS),
        out_shape=[
            pltpu.VMEM((SIZES[0], depth), BF16),
            jax.ShapeDtypeStruct((half, depth), BF16),
            jax.ShapeDtypeStruct((2 * owned, depth), BF16),
            jax.ShapeDtypeStruct((owned, half), F32),
            jax.ShapeDtypeStruct((half, 1), F32),
        ]
        + [jax.ShapeDtypeStruct((1, size), F32) for size in SIZES],
        scratch_shapes=[
            pltpu.VMEM(factors.shape, F32),
            pltpu.VMEM(weights.shape, F32),
            pltpu.SMEM(counts.shape, jnp.int32),
            pltpu.SemaphoreType.DMA,
            pltpu.SemaphoreType.DMA((2,)),
            pltpu.SemaphoreType.DMA((LOADS,)),
        ],
        compiler_params=PARAMS,
        cost_estimate=pl.CostEstimate(
            flops=0, bytes_accessed=4 * SIZES[0] * depth, transcendentals=0
        ),
        name="load",
    )(in_hbm(counts), in_hbm(weights), packed, in_hbm(factors), in_hbm(samples))


def cube_kernel(scale, value, passed, out):
    slots = value.shape[1]
    total = value[...] + passed[:, :slots].astype(F32)
    out[...] = (scale[...] * (total * total * total)).astype(BF16)


def cube(scale, value, passed):
    return pl.pallas_call(
        cube_kernel,
        in_specs=[VMEM] * 3,
        out_specs=VMEM,
        out_shape=jax.ShapeDtypeStruct(value.shape, BF16),
        compiler_params=PARAMS,
        cost_estimate=pl.CostEstimate(
            flops=4 * value.size, bytes_accessed=8 * value.size, transcendentals=0
        ),
        name="cube",
    )(scale, value, passed)


def nt_dot(left, right):
    return lax.dot_general(left, right, (((1,), (1,)), ((), ())), preferred_element_type=F32)


def project_part(mask, other, own, near, sent, kept, scratch):
    half, slots = kept.shape
    block = half // 2
    for i, quarter in enumerate(order_of()):
        at = pl.ds(pl.multiple_of((quarter >> 1) * block, block), block)
        to = slice(i * block, (i + 1) * block)
        for side, ref in enumerate((other, own)):

            @pl.when(quarter & 1 == side)
            def _():
                scratch[to, :] = ref[at, :]

    value = nt_dot(scratch[...], near[...])
    value = value * mask[...]
    sent[:, :slots] = value[:half].astype(BF16)
    kept[...] = value[half:]


def put_gram(sent, gram):
    slots = sent.shape[1] - LANES
    message = folded(gram_message(gram[...]).astype(F32)).astype(BF16)
    sent[:32, slots:] = message
    sent[32:, slots:] = jnp.zeros((sent.shape[0] - 32, LANES), BF16)


def first_kernel(mask, packed, own, left, gram_own, near, samples, sent, kept, other, gram, later, scratch, sems):
    copies = fetch(samples, later, sems, 1)
    unpack(packed, other, 0)
    project_part(mask, other, own, near, sent, kept, scratch)
    gram[...] = jnp.concatenate([gram_of(nt_dot(left[...], other[...])), gram_own[...]], 1)
    if GRAM_PART == 0:
        put_gram(sent, gram)
    for copy in copies:
        copy.wait()


def project_first(mask, packed, own, left, gram_own, near, samples):
    slots, depth = near.shape
    count = 2 * own.shape[0]
    return pl.pallas_call(
        first_kernel,
        in_specs=[VMEM] * 6 + [ANY],
        out_specs=[VMEM] * 5,
        out_shape=[
            jax.ShapeDtypeStruct((count // 2, slots + LANES * (GRAM_PART == 0)), BF16),
            jax.ShapeDtypeStruct((count // 2, slots), F32),
            jax.ShapeDtypeStruct((count // 2, depth), BF16),
            jax.ShapeDtypeStruct((left.shape[0] // 2, count), F32),
            pltpu.VMEM((SIZES[1], depth), BF16),
        ],
        scratch_shapes=[
            pltpu.VMEM((count, depth), BF16),
            pltpu.SemaphoreType.DMA((LOADS,)),
        ],
        compiler_params=PARAMS,
        cost_estimate=estimate(slots, depth, count),
        name="project_first",
    )(mask, packed, own, left, gram_own, in_vmem(near), in_hbm(samples))


def second_kernel(mask, other, own, gram, near, sent, kept, scratch):
    project_part(mask, other, own, near, sent, kept, scratch)
    if GRAM_PART == 1:
        put_gram(sent, gram)


def project_second(mask, other, own, gram, near):
    slots, depth = near.shape
    count = 2 * own.shape[0]
    return pl.pallas_call(
        second_kernel,
        in_specs=[VMEM] * 5,
        out_specs=[VMEM] * 2,
        out_shape=[
            jax.ShapeDtypeStruct((count // 2, slots + LANES * (GRAM_PART == 1)), BF16),
            jax.ShapeDtypeStruct((count // 2, slots), F32),
        ],
        scratch_shapes=[pltpu.VMEM((count, depth), BF16)],
        compiler_params=PARAMS,
        cost_estimate=estimate(slots, depth, count),
        name="project_second",
    )(mask, other, own, gram, in_vmem(near))


def estimate(slots, depth, rows):
    return pl.CostEstimate(
        flops=2 * slots * depth * rows, bytes_accessed=2 * slots * depth, transcendentals=0
    )


def model_kernel(counts, weights, gram, other, own, factors, out, inverse):
    _, _, core, chip = place_of()
    owned, count = gram.shape
    half = count // 2
    row = weights[...].reshape(1, count)
    column = chosen(row, number(lax.broadcasted_iota(jnp.int32, (count, 1), 0), count, core))
    down = lax.broadcasted_iota(jnp.int32, (count, count), 0)
    along = lax.broadcasted_iota(jnp.int32, (count, count), 1)
    weight = jnp.sum(jnp.where(down == along, column, 0.0), 0, keepdims=True)
    mine = half + chip * owned + lax.broadcasted_iota(jnp.int32, (owned, 1), 0)
    pairs = chosen(row, number(mine, count, core)) * weight
    value = pairs * gram[...] * gram[...] * gram[...]
    lanes = lax.broadcasted_iota(jnp.int32, (owned, count), 1)
    diagonal = jnp.sum(jnp.where(lanes == mine, value, 0.0), 1, keepdims=True)
    left = gram_message(value)
    both = jnp.dot(left[:, :half], other[...], preferred_element_type=F32) + jnp.dot(
        left[:, half:], own[...], preferred_element_type=F32
    )
    rest = factors[...] - factors[...].astype(BF16).astype(F32)
    out[...] = 8.0 * (gram_of(both) + diagonal * rest)
    total = counts[0]
    for i in range(1, N_DP):
        total = total + counts[i]
    inverse[...] = 8.0 / jnp.full(inverse.shape, total, jnp.int32).astype(F32)


def model(counts, weights, gram, other, own, factors):
    return pl.pallas_call(
        model_kernel,
        in_specs=[SMEM] + [VMEM] * 5,
        out_specs=[VMEM] * 2,
        out_shape=[
            jax.ShapeDtypeStruct(factors.shape, F32),
            jax.ShapeDtypeStruct((1, factors.shape[1]), F32),
        ],
        compiler_params=PARAMS,
        name="model",
    )(counts, weights, gram, other, own, factors)


def finish_kernel(blocks, model_term, inverse, out):
    rows, width = model_term.shape[0], blocks.shape[1]
    total = jnp.zeros((2 * rows, width), F32)
    for chip in range(CHIPS):
        total = total + blocks[pl.ds(16 * chip, 16), :].astype(F32)
    total = jnp.concatenate([total[:rows], total[rows:]], 1)
    out[...] = model_term[...] - inverse[...] * total


def finish(blocks, model_term, inverse):
    return pl.pallas_call(
        finish_kernel,
        in_specs=[VMEM] * 3,
        out_specs=VMEM,
        out_shape=jax.ShapeDtypeStruct(model_term.shape, F32),
        compiler_params=PARAMS,
        name="finish",
    )(blocks, model_term, inverse)


def cross_kernel(mine, other, near, *refs, sides, add, tile):
    terms, refs = (refs[: len(sides)] if add else None), refs[add * len(sides) :]
    outs, rows = refs[:-1], refs[-1]
    block = mine.shape[0] // 2
    half = 2 * block
    pieces = (other[:block], other[block:], mine[:block], mine[block:])
    for quarter, piece in zip(order_of(), pieces):
        at = pl.multiple_of((quarter & 1) * half + (quarter >> 1) * block, block)
        rows[pl.ds(at, block), :] = piece
    width = outs[0].shape[1]
    first = sides[0] * half
    used = slice(first, first + len(sides) * half)

    @pl.loop(0, width // tile)
    def _(i):
        here = pl.ds(pl.multiple_of(i * tile, tile), tile)
        there = pl.ds(pl.multiple_of(width + i * tile, tile), tile)
        left, right = (
            jnp.dot(rows[used, :], near[:, at], preferred_element_type=F32) for at in (here, there)
        )
        for place, out in enumerate(outs):
            for chip in range(CHIPS):
                at = place * half + 8 * chip
                to = slice(16 * chip, 16 * chip + 16)
                value = jnp.concatenate([left[at : at + 8], right[at : at + 8]], 0)
                if add:
                    value = value + terms[place][to, here]
                out[to, here] = value.astype(out.dtype)


def cross(pieces, near, sides, out_type, terms=(), tile=1024):
    slots, depth = near.shape
    rows = 2 * pieces[0].shape[0]
    out = jax.ShapeDtypeStruct((rows, depth // 2), out_type)
    return pl.pallas_call(
        functools.partial(cross_kernel, sides=sides, add=bool(terms), tile=tile),
        in_specs=[VMEM] * (3 + len(terms)),
        out_specs=[VMEM] * len(sides),
        out_shape=[out] * len(sides),
        scratch_shapes=[pltpu.VMEM((rows, slots), BF16)],
        compiler_params=PARAMS,
        cost_estimate=estimate(slots, depth, rows),
        name="cross",
    )(*pieces, in_vmem(near), *terms)


def pair_kernel(piece, near, term_other, term_own, out_other, out_own, rows, *, first, tile):
    block = piece.shape[0] // 2
    pair = order_of()[first : first + 2]
    for i, quarter in enumerate(pair):
        at = pl.multiple_of((quarter & 1) * block, block)
        rows[pl.ds(at, block), :] = piece[i * block : (i + 1) * block, : rows.shape[1]]
    swapped = pair[0] & 1 == 1
    tops = [
        pl.multiple_of((jnp.where(swapped, pair[1 - i], pair[i]) >> 1) * 2 * block, 2 * block)
        for i in range(2)
    ]
    width = out_own.shape[1]

    @pl.loop(0, width // tile)
    def _(i):
        here = pl.ds(pl.multiple_of(i * tile, tile), tile)
        there = pl.ds(pl.multiple_of(width + i * tile, tile), tile)
        left, right = (
            jnp.dot(rows[...], near[:, at], preferred_element_type=F32) for at in (here, there)
        )
        for side, (out, term) in enumerate(((out_other, term_other), (out_own, term_own))):
            for chip in range(CHIPS // 2):
                at = side * block + 8 * chip
                to = slice(16 * chip, 16 * chip + 16)
                value = jnp.concatenate([left[at : at + 8], right[at : at + 8]], 0)
                value = value + term[pl.ds(tops[side] + 16 * chip, 16), here]
                out[to, here] = value.astype(out.dtype)


def cross_pair(piece, near, terms, first, kind, tile=1024):
    slots, depth = near.shape
    rows = piece.shape[0]
    return pl.pallas_call(
        functools.partial(pair_kernel, first=first, tile=tile),
        in_specs=[VMEM] * 4,
        out_specs=[VMEM] * 2,
        out_shape=[
            jax.ShapeDtypeStruct((rows, depth // 2), kind),
            jax.ShapeDtypeStruct((rows, depth // 2), F32),
        ],
        scratch_shapes=[pltpu.VMEM((rows, slots), BF16)],
        compiler_params=PARAMS,
        cost_estimate=estimate(slots, depth, rows),
        name="cross_pair",
    )(piece, in_vmem(near), *terms)


def add_kernel(kept, sent, from_kept, from_sent, out):
    half = kept.shape[0]
    _, _, core, _ = place_of()
    pair = order_of()[2:]
    mine = jnp.where(pair[0] & 1 == 1, pair[0], pair[1]) >> 1
    pair = order_of(1 - core)[2:]
    theirs = jnp.where(pair[0] & 1 == 0, pair[0], pair[1]) >> 1
    for i in range(2):
        own = jnp.where(mine == i, kept[...], sent[...])
        other = jnp.where(theirs == i, from_kept[...].astype(F32), from_sent[...].astype(F32))
        out[i * half : (i + 1) * half, :] = (own + other).astype(BF16)


def add(kept, sent, from_kept, from_sent):
    return pl.pallas_call(
        add_kernel,
        in_specs=[VMEM] * 4,
        out_specs=VMEM,
        out_shape=pltpu.VMEM((2 * kept.shape[0], kept.shape[1]), BF16),
        compiler_params=PARAMS,
        name="add",
    )(kept, sent, from_kept, from_sent)


def on_device(samples, factors, weights, counts):
    owned, depth = factors.shape
    packed_own = plane_exchange(spread(factors))
    near0, own, left, gram_own, scale, mask0, mask1 = load(
        counts, weights, packed_own, factors, samples
    )
    packed_other = core_swap(packed_own)
    sent0, kept0, other, gram, near1 = project_first(
        mask0, packed_other, own, left, gram_own, near0, samples
    )
    sent1, kept1 = project_second(mask1, other, own, gram, near1)
    nears = (near0, near1)

    pieces = []
    for part, (sent, kept) in enumerate(((sent0, kept0), (sent1, kept1))):
        slots = kept.shape[1]
        carries = part == GRAM_PART
        with jax.named_scope(f"halves{part}"):
            got = feat_swap(sent, partner_first)
        value = kept + got[:, :slots].astype(F32)
        message = value.astype(BF16)
        if carries:
            gram = gram + gram_from(got[:32, slots:])
            high = lax.reduce_precision(gram, 8, 7)
            extra = folded(jnp.concatenate([high, gram - high], 0)).astype(BF16)
            extra = jnp.pad(extra, ((0, kept.shape[0] - 32), (0, 0)))
            message = jnp.concatenate([message, extra], 1)
        with jax.named_scope(f"sums{part}"):
            passed = feat_swap(message, partner_second)
        if carries:
            gram = gram + gram_from(passed[:32, slots:])
        if part == PARTS - 1:
            model_term, inverse = model(counts, weights, gram, other, own, factors)
            scale, model_term, inverse = lax.optimization_barrier((scale, model_term, inverse))
        cubes = cube(scale, value, passed)
        with jax.named_scope(f"cubes{part}"):
            pieces.append((cubes, feat_swap(cubes, partner_first)))

    terms = ()
    for part in range(PARTS - 1):
        terms = cross(pieces[part], nears[part], (0, 1), F32, terms)
    cubes, got = pieces[-1]
    other_kept, own_kept = cross_pair(cubes, nears[-1], terms, 2, F32)
    from_kept = core_swap(other_kept)
    other_sent, own_sent = cross_pair(got, nears[-1], terms, 0, BF16)
    total_own = add(own_kept, own_sent, from_kept, core_swap(other_sent))

    return finish(plane_exchange(total_own), model_term, inverse)


def solution(mesh):
    in_specs = (P("dp", "feat"), P("dp", "feat"), P(), P())
    out_specs = P("dp", "feat")
    return jax.shard_map(
        on_device, mesh=mesh, in_specs=in_specs, out_specs=out_specs, check_vma=False
    )
```

```python
import functools

import jax
import jax.numpy as jnp
from jax import lax
from jax.experimental import pallas as pl
from jax.experimental.pallas import tpu as pltpu
from jax.sharding import PartitionSpec as P

BF16 = jnp.bfloat16
F32 = jnp.float32
N_DP = 32
N_FEAT = 4
CHIPS = N_DP // 2
SIZES = (1664, 1408)
GRAM_PART = 0
LANES = 128
PARTS = len(SIZES)
LOADS = 1
PLANES = [[2 * chip + core for chip in range(CHIPS)] for core in range(2)]
VMEM = pl.BlockSpec(memory_space=pltpu.VMEM)
SMEM = pl.BlockSpec(memory_space=pltpu.SMEM)
ANY = pl.BlockSpec(memory_space=pl.ANY)
PARAMS = pltpu.CompilerParams(vmem_limit_bytes=8 << 20)


def in_hbm(array):
    return pltpu.with_memory_space_constraint(array, pltpu.HBM)


def in_vmem(array):
    return pltpu.with_memory_space_constraint(array, pltpu.VMEM)


def partner_first(core, y):
    return y ^ 1 if core == 0 else 3 - y


def partner_second(core, y):
    return 3 - y if core == 0 else y ^ 1


PARTNERS = (partner_first, partner_second)


def feat_swap(x, partner):
    pairs = []
    for dp in range(N_DP):
        for y in range(N_FEAT):
            pairs.append((dp * N_FEAT + y, dp * N_FEAT + partner(dp % 2, y)))
    return lax.ppermute(x, ("dp", "feat"), pairs)


def core_swap(x):
    return lax.ppermute(x, "dp", [(i, i ^ 1) for i in range(N_DP)])


def plane_exchange(x):
    return lax.all_to_all(x, "dp", 0, 0, axis_index_groups=PLANES, tiled=True)


def spread_kernel(factors, out):
    width = out.shape[1]
    block = jnp.concatenate([factors[:, :width], factors[:, width:]], 0).astype(BF16)
    for chip in range(CHIPS):
        out[pl.ds(16 * chip, 16), :] = block


def spread(factors):
    return pl.pallas_call(
        spread_kernel,
        in_specs=[VMEM],
        out_specs=VMEM,
        out_shape=pltpu.VMEM((16 * CHIPS, factors.shape[1] // 2), BF16),
        compiler_params=PARAMS,
        name="spread",
    )(in_hbm(factors))


def unpack(packed, out, top):
    for pair in range(CHIPS // 2):
        block = packed[pl.ds(32 * pair, 32), :].astype(F32)
        upper = jnp.concatenate([block[:8], block[8:16]], 1)
        lower = jnp.concatenate([block[16:24], block[24:]], 1)
        out[pl.ds(top + 16 * pair, 16), :] = jnp.concatenate([upper, lower], 0).astype(BF16)


def parts_of(value):
    high = value.astype(BF16)
    return high, (value - high.astype(F32)).astype(BF16)


def gram_message(gram):
    return jnp.concatenate([part.astype(F32) for part in parts_of(gram)], 0).astype(BF16)


def gram_of(message):
    value = message.astype(F32)
    return value[:8] + value[8:16]


def folded(value):
    return jnp.concatenate([value[:, :LANES], value[:, LANES:]], 0)


def gram_from(message):
    value = message.astype(F32)
    return jnp.concatenate([gram_of(value[:16]), gram_of(value[16:32])], 1)


def start_of(part):
    return sum(SIZES[:part])


def fetch(samples, near, sems, part):
    rows = SIZES[part] // LOADS
    copies = []
    for i in range(LOADS):
        here = pl.ds(i * rows, rows)
        there = pl.ds(start_of(part) + i * rows, rows)
        copies.append(pltpu.make_async_copy(samples.at[there, :], near.at[here, :], sems.at[i]))
        copies[-1].start()
    return copies


def place_of():
    dp = lax.axis_index("dp")
    return dp, lax.axis_index("feat"), dp & 1, dp >> 1


def order_of(core=None):
    _, y, mine, _ = place_of()
    core = mine if core is None else core
    first = jnp.where(core == 0, y ^ 1, 3 - y)
    second = jnp.where(core == 0, 3 - y, y ^ 1)
    order = []
    for pair in ((first, y ^ 2), (y, second)):
        order += [jnp.minimum(*pair), jnp.maximum(*pair)]
    return order


def chosen(weights, numbers):
    lanes = lax.broadcasted_iota(jnp.int32, (numbers.shape[0], weights.shape[1]), 1)
    return jnp.sum(jnp.where(lanes == numbers, weights, 0.0), 1, keepdims=True)


def number(place, count, core):
    half = count // 2
    inside = place & (half - 1)
    side = jnp.where(place < half, 1 - core, core)
    return (inside >> 3) * 16 + side * 8 + (inside & 7)


def load_kernel(counts, weights, packed, factors, samples, *refs):
    near, rows, left, gram, scale, *masks, mine, row, numbers, sem, small, sems = refs
    first = pltpu.make_async_copy(factors, mine, sem)
    first.start()
    others = [
        pltpu.make_async_copy(weights, row, small.at[0]),
        pltpu.make_async_copy(counts, numbers, small.at[1]),
    ]
    for copy in others:
        copy.start()
    copies = fetch(samples, near, sems, 0)
    unpack(packed, rows, 0)
    first.wait()
    left[...] = gram_message(mine[...])
    gram[...] = gram_of(nt_dot(left[...], rows[...]))
    for copy in others:
        copy.wait()
    order = order_of()
    dp, _, core, _ = place_of()
    for part, mask in enumerate(masks):
        slot = start_of(part) + lax.broadcasted_iota(jnp.int32, mask.shape, 1)
        mask[...] = jnp.where(slot < numbers[dp], 1.0, 0.0)
    half = scale.shape[0]
    block = half // 2
    step = lax.broadcasted_iota(jnp.int32, (half, 1), 0)
    tops = [(quarter & 1) * half + (quarter >> 1) * block for quarter in order[2:]]
    at = jnp.where(step < block, tops[0] + step, tops[1] + step - block)
    scale[...] = chosen(row[...].reshape(1, 2 * half), number(at, 2 * half, core))
    for copy in copies:
        copy.wait()


def load(counts, weights, packed, factors, samples):
    depth = samples.shape[1]
    owned = factors.shape[0]
    half = packed.shape[0] // 2
    return pl.pallas_call(
        load_kernel,
        in_specs=[ANY, ANY, VMEM, ANY, ANY],
        out_specs=[VMEM] * (5 + PARTS),
        out_shape=[
            pltpu.VMEM((SIZES[0], depth), BF16),
            jax.ShapeDtypeStruct((half, depth), BF16),
            jax.ShapeDtypeStruct((2 * owned, depth), BF16),
            jax.ShapeDtypeStruct((owned, half), F32),
            jax.ShapeDtypeStruct((half, 1), F32),
        ]
        + [jax.ShapeDtypeStruct((1, size), F32) for size in SIZES],
        scratch_shapes=[
            pltpu.VMEM(factors.shape, F32),
            pltpu.VMEM(weights.shape, F32),
            pltpu.SMEM(counts.shape, jnp.int32),
            pltpu.SemaphoreType.DMA,
            pltpu.SemaphoreType.DMA((2,)),
            pltpu.SemaphoreType.DMA((LOADS,)),
        ],
        compiler_params=PARAMS,
        cost_estimate=pl.CostEstimate(
            flops=0, bytes_accessed=4 * SIZES[0] * depth, transcendentals=0
        ),
        name="load",
    )(in_hbm(counts), in_hbm(weights), packed, in_hbm(factors), in_hbm(samples))


def cube_kernel(scale, value, passed, out):
    slots = value.shape[1]
    total = value[...] + passed[:, :slots].astype(F32)
    out[...] = (scale[...] * (total * total * total)).astype(BF16)


def cube(scale, value, passed):
    return pl.pallas_call(
        cube_kernel,
        in_specs=[VMEM] * 3,
        out_specs=VMEM,
        out_shape=jax.ShapeDtypeStruct(value.shape, BF16),
        compiler_params=PARAMS,
        cost_estimate=pl.CostEstimate(
            flops=4 * value.size, bytes_accessed=8 * value.size, transcendentals=0
        ),
        name="cube",
    )(scale, value, passed)


def nt_dot(left, right):
    return lax.dot_general(left, right, (((1,), (1,)), ((), ())), preferred_element_type=F32)


def arrange(other, own, scratch):
    block = scratch.shape[0] // 4
    for i, quarter in enumerate(order_of()):
        at = pl.ds(pl.multiple_of((quarter >> 1) * block, block), block)
        to = slice(i * block, (i + 1) * block)
        for side, ref in enumerate((other, own)):

            @pl.when(quarter & 1 == side)
            def _():
                scratch[to, :] = ref[at, :]


def project_part(mask, near, sent, kept, scratch):
    half, slots = kept.shape
    value = nt_dot(scratch[...], near[...])
    value = value * mask[...]
    sent[:, :slots] = value[:half].astype(BF16)
    kept[...] = value[half:]


def put_gram(sent, gram):
    slots = sent.shape[1] - LANES
    message = folded(gram_message(gram[...]).astype(F32)).astype(BF16)
    sent[:32, slots:] = message
    sent[32:, slots:] = jnp.zeros((sent.shape[0] - 32, LANES), BF16)


def first_kernel(mask, packed, own, left, gram_own, near, samples, sent, kept, other, gram, later, scratch, sems):
    copies = fetch(samples, later, sems, 1)
    unpack(packed, other, 0)
    arrange(other, own, scratch)
    project_part(mask, near, sent, kept, scratch)
    gram[...] = jnp.concatenate([gram_of(nt_dot(left[...], other[...])), gram_own[...]], 1)
    if GRAM_PART == 0:
        put_gram(sent, gram)
    for copy in copies:
        copy.wait()


def project_first(mask, packed, own, left, gram_own, near, samples):
    slots, depth = near.shape
    count = 2 * own.shape[0]
    return pl.pallas_call(
        first_kernel,
        in_specs=[VMEM] * 6 + [ANY],
        out_specs=[VMEM] * 6,
        out_shape=[
            jax.ShapeDtypeStruct((count // 2, slots + LANES * (GRAM_PART == 0)), BF16),
            jax.ShapeDtypeStruct((count // 2, slots), F32),
            jax.ShapeDtypeStruct((count // 2, depth), BF16),
            jax.ShapeDtypeStruct((left.shape[0] // 2, count), F32),
            pltpu.VMEM((SIZES[1], depth), BF16),
            jax.ShapeDtypeStruct((count, depth), BF16),
        ],
        scratch_shapes=[
            pltpu.SemaphoreType.DMA((LOADS,)),
        ],
        compiler_params=PARAMS,
        cost_estimate=estimate(slots, depth, count),
        name="project_first",
    )(mask, packed, own, left, gram_own, in_vmem(near), in_hbm(samples))


def second_kernel(mask, scratch, gram, near, sent, kept):
    project_part(mask, near, sent, kept, scratch)
    if GRAM_PART == 1:
        put_gram(sent, gram)


def project_second(mask, rows, gram, near):
    slots, depth = near.shape
    count = rows.shape[0]
    return pl.pallas_call(
        second_kernel,
        in_specs=[VMEM] * 4,
        out_specs=[VMEM] * 2,
        out_shape=[
            jax.ShapeDtypeStruct((count // 2, slots + LANES * (GRAM_PART == 1)), BF16),
            jax.ShapeDtypeStruct((count // 2, slots), F32),
        ],
        compiler_params=PARAMS,
        cost_estimate=estimate(slots, depth, count),
        name="project_second",
    )(mask, rows, gram, in_vmem(near))


def estimate(slots, depth, rows):
    return pl.CostEstimate(
        flops=2 * slots * depth * rows, bytes_accessed=2 * slots * depth, transcendentals=0
    )


def model_kernel(counts, weights, gram, other, own, factors, out, inverse):
    _, _, core, chip = place_of()
    owned, count = gram.shape
    half = count // 2
    row = weights[...].reshape(1, count)
    column = chosen(row, number(lax.broadcasted_iota(jnp.int32, (count, 1), 0), count, core))
    down = lax.broadcasted_iota(jnp.int32, (count, count), 0)
    along = lax.broadcasted_iota(jnp.int32, (count, count), 1)
    weight = jnp.sum(jnp.where(down == along, column, 0.0), 0, keepdims=True)
    mine = half + chip * owned + lax.broadcasted_iota(jnp.int32, (owned, 1), 0)
    pairs = chosen(row, number(mine, count, core)) * weight
    value = pairs * gram[...] * gram[...] * gram[...]
    lanes = lax.broadcasted_iota(jnp.int32, (owned, count), 1)
    diagonal = jnp.sum(jnp.where(lanes == mine, value, 0.0), 1, keepdims=True)
    left = gram_message(value)
    both = jnp.dot(left[:, :half], other[...], preferred_element_type=F32) + jnp.dot(
        left[:, half:], own[...], preferred_element_type=F32
    )
    rest = factors[...] - factors[...].astype(BF16).astype(F32)
    out[...] = 8.0 * (gram_of(both) + diagonal * rest)
    total = counts[0]
    for i in range(1, N_DP):
        total = total + counts[i]
    inverse[...] = 8.0 / jnp.full(inverse.shape, total, jnp.int32).astype(F32)


def model(counts, weights, gram, other, own, factors):
    return pl.pallas_call(
        model_kernel,
        in_specs=[SMEM] + [VMEM] * 5,
        out_specs=[VMEM] * 2,
        out_shape=[
            jax.ShapeDtypeStruct(factors.shape, F32),
            jax.ShapeDtypeStruct((1, factors.shape[1]), F32),
        ],
        compiler_params=PARAMS,
        name="model",
    )(counts, weights, gram, other, own, factors)


def finish_kernel(blocks, model_term, inverse, out):
    rows, width = model_term.shape[0], blocks.shape[1]
    total = jnp.zeros((2 * rows, width), F32)
    for chip in range(CHIPS):
        total = total + blocks[pl.ds(16 * chip, 16), :].astype(F32)
    total = jnp.concatenate([total[:rows], total[rows:]], 1)
    out[...] = model_term[...] - inverse[...] * total


def finish(blocks, model_term, inverse):
    return pl.pallas_call(
        finish_kernel,
        in_specs=[VMEM] * 3,
        out_specs=VMEM,
        out_shape=jax.ShapeDtypeStruct(model_term.shape, F32),
        compiler_params=PARAMS,
        name="finish",
    )(blocks, model_term, inverse)


def cross_kernel(mine, other, near, *refs, sides, add, tile):
    terms, refs = (refs[: len(sides)] if add else None), refs[add * len(sides) :]
    outs, rows = refs[:-1], refs[-1]
    block = mine.shape[0] // 2
    half = 2 * block
    pieces = (other[:block], other[block:], mine[:block], mine[block:])
    for quarter, piece in zip(order_of(), pieces):
        at = pl.multiple_of((quarter & 1) * half + (quarter >> 1) * block, block)
        rows[pl.ds(at, block), :] = piece
    width = outs[0].shape[1]
    first = sides[0] * half
    used = slice(first, first + len(sides) * half)

    @pl.loop(0, width // tile)
    def _(i):
        here = pl.ds(pl.multiple_of(i * tile, tile), tile)
        there = pl.ds(pl.multiple_of(width + i * tile, tile), tile)
        left, right = (
            jnp.dot(rows[used, :], near[:, at], preferred_element_type=F32) for at in (here, there)
        )
        for place, out in enumerate(outs):
            for chip in range(CHIPS):
                at = place * half + 8 * chip
                to = slice(16 * chip, 16 * chip + 16)
                value = jnp.concatenate([left[at : at + 8], right[at : at + 8]], 0)
                if add:
                    value = value + terms[place][to, here]
                out[to, here] = value.astype(out.dtype)


def cross(pieces, near, sides, out_type, terms=(), tile=1024):
    slots, depth = near.shape
    rows = 2 * pieces[0].shape[0]
    out = jax.ShapeDtypeStruct((rows, depth // 2), out_type)
    return pl.pallas_call(
        functools.partial(cross_kernel, sides=sides, add=bool(terms), tile=tile),
        in_specs=[VMEM] * (3 + len(terms)),
        out_specs=[VMEM] * len(sides),
        out_shape=[out] * len(sides),
        scratch_shapes=[pltpu.VMEM((rows, slots), BF16)],
        compiler_params=PARAMS,
        cost_estimate=estimate(slots, depth, rows),
        name="cross",
    )(*pieces, in_vmem(near), *terms)


def pair_kernel(piece, near, term_other, term_own, out_other, out_own, rows, *, first, tile):
    block = piece.shape[0] // 2
    pair = order_of()[first : first + 2]
    for i, quarter in enumerate(pair):
        at = pl.multiple_of((quarter & 1) * block, block)
        rows[pl.ds(at, block), :] = piece[i * block : (i + 1) * block, : rows.shape[1]]
    swapped = pair[0] & 1 == 1
    tops = [
        pl.multiple_of((jnp.where(swapped, pair[1 - i], pair[i]) >> 1) * 2 * block, 2 * block)
        for i in range(2)
    ]
    width = out_own.shape[1]

    @pl.loop(0, width // tile)
    def _(i):
        here = pl.ds(pl.multiple_of(i * tile, tile), tile)
        there = pl.ds(pl.multiple_of(width + i * tile, tile), tile)
        left, right = (
            jnp.dot(rows[...], near[:, at], preferred_element_type=F32) for at in (here, there)
        )
        for side, (out, term) in enumerate(((out_other, term_other), (out_own, term_own))):
            for chip in range(CHIPS // 2):
                at = side * block + 8 * chip
                to = slice(16 * chip, 16 * chip + 16)
                value = jnp.concatenate([left[at : at + 8], right[at : at + 8]], 0)
                value = value + term[pl.ds(tops[side] + 16 * chip, 16), here]
                out[to, here] = value.astype(out.dtype)


def cross_pair(piece, near, terms, first, kind, tile=1024):
    slots, depth = near.shape
    rows = piece.shape[0]
    return pl.pallas_call(
        functools.partial(pair_kernel, first=first, tile=tile),
        in_specs=[VMEM] * 4,
        out_specs=[VMEM] * 2,
        out_shape=[
            jax.ShapeDtypeStruct((rows, depth // 2), kind),
            jax.ShapeDtypeStruct((rows, depth // 2), F32),
        ],
        scratch_shapes=[pltpu.VMEM((rows, slots), BF16)],
        compiler_params=PARAMS,
        cost_estimate=estimate(slots, depth, rows),
        name="cross_pair",
    )(piece, in_vmem(near), *terms)


def add_kernel(kept, sent, from_kept, from_sent, out):
    half = kept.shape[0]
    _, _, core, _ = place_of()
    pair = order_of()[2:]
    mine = jnp.where(pair[0] & 1 == 1, pair[0], pair[1]) >> 1
    pair = order_of(1 - core)[2:]
    theirs = jnp.where(pair[0] & 1 == 0, pair[0], pair[1]) >> 1
    for i in range(2):
        own = jnp.where(mine == i, kept[...], sent[...])
        other = jnp.where(theirs == i, from_kept[...].astype(F32), from_sent[...].astype(F32))
        out[i * half : (i + 1) * half, :] = (own + other).astype(BF16)


def add(kept, sent, from_kept, from_sent):
    return pl.pallas_call(
        add_kernel,
        in_specs=[VMEM] * 4,
        out_specs=VMEM,
        out_shape=pltpu.VMEM((2 * kept.shape[0], kept.shape[1]), BF16),
        compiler_params=PARAMS,
        name="add",
    )(kept, sent, from_kept, from_sent)


def on_device(samples, factors, weights, counts):
    owned, depth = factors.shape
    packed_own = plane_exchange(spread(factors))
    near0, own, left, gram_own, scale, mask0, mask1 = load(
        counts, weights, packed_own, factors, samples
    )
    packed_other = core_swap(packed_own)
    sent0, kept0, other, gram, near1, rows = project_first(
        mask0, packed_other, own, left, gram_own, near0, samples
    )
    sent1, kept1 = project_second(mask1, rows, gram, near1)
    nears = (near0, near1)

    pieces = []
    for part, (sent, kept) in enumerate(((sent0, kept0), (sent1, kept1))):
        slots = kept.shape[1]
        carries = part == GRAM_PART
        with jax.named_scope(f"halves{part}"):
            got = feat_swap(sent, partner_first)
        value = kept + got[:, :slots].astype(F32)
        message = value.astype(BF16)
        if carries:
            gram = gram + gram_from(got[:32, slots:])
            high = lax.reduce_precision(gram, 8, 7)
            extra = folded(jnp.concatenate([high, gram - high], 0)).astype(BF16)
            extra = jnp.pad(extra, ((0, kept.shape[0] - 32), (0, 0)))
            message = jnp.concatenate([message, extra], 1)
        with jax.named_scope(f"sums{part}"):
            passed = feat_swap(message, partner_second)
        if carries:
            gram = gram + gram_from(passed[:32, slots:])
        if part == PARTS - 1:
            model_term, inverse = model(counts, weights, gram, other, own, factors)
            scale, model_term, inverse = lax.optimization_barrier((scale, model_term, inverse))
        cubes = cube(scale, value, passed)
        with jax.named_scope(f"cubes{part}"):
            pieces.append((cubes, feat_swap(cubes, partner_first)))

    terms = ()
    for part in range(PARTS - 1):
        terms = cross(pieces[part], nears[part], (0, 1), F32, terms)
    cubes, got = pieces[-1]
    other_kept, own_kept = cross_pair(cubes, nears[-1], terms, 2, F32)
    from_kept = core_swap(other_kept)
    other_sent, own_sent = cross_pair(got, nears[-1], terms, 0, BF16)
    total_own = add(own_kept, own_sent, from_kept, core_swap(other_sent))

    return finish(plane_exchange(total_own), model_term, inverse)


def solution(mesh):
    in_specs = (P("dp", "feat"), P("dp", "feat"), P(), P())
    out_specs = P("dp", "feat")
    return jax.shard_map(
        on_device, mesh=mesh, in_specs=in_specs, out_specs=out_specs, check_vma=False
    )
```
